32 devices in a mesh: dp: 8 (over z, x), group: 2 (over core), mp: 2 (over y).
Axes of the slice: x: 2, y: 2, z: 4, core: 2. Of those that a mesh axis runs over, the one named last changes fastest.
Arguments:
- teacher_rows: bfloat16 [5120, 5120], P('dp', ('group', 'mp')), may hold values from -500 to 500
- teacher_gain: bfloat16 [5120], P(('group', 'mp')), may hold values from 0.099609375 to 1.8984375
- teacher_head: bfloat16 [1536, 5120], P(('group', 'mp'), 'dp'), may hold values from -3 to 3
- student_rows: bfloat16 [5120, 2048], P('dp'), may hold values from -500 to 500
- student_gain: bfloat16 [2048], replicated, may hold values from 0.099609375 to 1.8984375
- student_head: bfloat16 [1536, 2048], P(('group', 'mp'), 'dp'), may hold values from -3 to 3
- lengths: int32 [8], P('dp'), may hold values from 384 to 640, as said below
Outputs:
- head_update: bfloat16 [1536, 2048], P(('group', 'mp'), 'dp')
- row_update: bfloat16 [5120, 2048], P(('dp', 'group', 'mp'))
The draws below stay inside these ranges and needn't reach their ends.
Inputs may be any that keep to these rules, and one draw needn't show every extreme that they name: `lengths`: the first sequence has exactly 384 tokens and the last exactly 640.
All inputs are finite; a program needn't handle non-finite values.
Results may differ from the reference program's by a relative error of at most 0.023.
Values may be sent and summed in bfloat16 or wider, within the bound.
A program may use at most 64 MiB of HBM per device.

```python
import math
import jax
import jax.numpy as jnp
from jax import lax

DT = 5120
DS = 2048
VOC_DEV = 384
LMAX = 640
SEQ_DEV = 1
TOK_DEV = 640
SEQUENCES = 8
TOKENS = 5120
VOCAB = 1536
N_DP = 8
N_GROUP = 2
N_MP = 2


def spread_scales(key, rows, cols):
    key_row, key_col = jax.random.split(key)
    row_scale = jnp.exp(jax.random.uniform(key_row, (rows, 1), minval=0.0, maxval=math.log(10.0)))
    col_scale = jnp.exp(jax.random.uniform(key_col, (1, cols), minval=0.0, maxval=math.log(10.0)))
    return row_scale * col_scale


def drawn_rows(key, width):
    key_value, key_scale = jax.random.split(key)
    values = jax.random.truncated_normal(key_value, -4.0, 4.0, (TOKENS, width))
    return values * spread_scales(key_scale, TOKENS, width)


def head_values(key, width):
    return jax.random.truncated_normal(key, -4.0, 4.0, (VOCAB, width)) * (3.0 / math.sqrt(width))


def draw_teacher_rows(key, part):
    key = jax.random.fold_in(key, 11)
    values = drawn_rows(key, DT)
    return values.astype(jnp.bfloat16)


def draw_teacher_head(key, part):
    key = jax.random.fold_in(key, 12)
    values = head_values(key, DT)
    return values.astype(jnp.bfloat16)


def draw_student_rows(key, part):
    key = jax.random.fold_in(key, 14)
    values = drawn_rows(key, DS)
    return values.astype(jnp.bfloat16)


def draw_student_head(key, part):
    key = jax.random.fold_in(key, 15)
    values = head_values(key, DS)
    return values.astype(jnp.bfloat16)


def draw_lengths(key, part):
    key = jax.random.fold_in(key, 13)
    shortest = 3 * LMAX // 5
    reach = LMAX // 8
    climb = 2 * LMAX // 5 - reach
    index = jnp.arange(SEQUENCES, dtype=jnp.int32)
    base = shortest + climb * index // SEQUENCES
    values = base + jax.random.randint(key, (SEQUENCES,), 0, reach + 1, dtype=jnp.int32)
    values = jnp.minimum(values, LMAX)
    values = values.at[0].set(shortest)
    return values.at[SEQUENCES - 1].set(LMAX)


def setup_inputs(seed: int = 0) -> dict:
    streams_of = jax.random.split(jax.random.key(seed), 8)
    return {
        "teacher_rows": draw_teacher_rows(jax.random.fold_in(streams_of[7], 71), 0),
        "teacher_gain": jnp.clip(1.0 + 0.18 * jax.random.normal(streams_of[1], (DT,), jnp.float32), 0.099609375, 1.8984375).astype(jnp.bfloat16),
        "teacher_head": draw_teacher_head(jax.random.fold_in(streams_of[7], 71), 0),
        "student_rows": draw_student_rows(jax.random.fold_in(streams_of[7], 71), 0),
        "student_gain": jnp.clip(1.0 + 0.18 * jax.random.normal(streams_of[4], (DS,), jnp.float32), 0.099609375, 1.8984375).astype(jnp.bfloat16),
        "student_head": draw_student_head(jax.random.fold_in(streams_of[7], 71), 0),
        "lengths": draw_lengths(jax.random.fold_in(streams_of[7], 71), 0),
    }


epsilon = 1e-06

def rms_rows(rows, gain):
    values = rows.astype(jnp.float32)
    mean_square = lax.optimization_barrier(jnp.mean(values * values, axis=-1, keepdims=True))
    return (values * lax.rsqrt(mean_square + epsilon) * gain.astype(jnp.float32)).astype(jnp.bfloat16)

def log_total(logits):
    highest = lax.optimization_barrier(jnp.max(logits, axis=1))
    return highest + jnp.log(lax.optimization_barrier(jnp.sum(jnp.exp(logits - highest[:, None]), axis=1)))

def to_bfloat(values):
    rounded = values.astype(jnp.bfloat16)
    rounded = lax.optimization_barrier(rounded)
    return rounded.astype(jnp.float32)

def reference(teacher_rows, teacher_gain, teacher_head, student_rows, student_gain, student_head, lengths):
    shards = N_GROUP * N_MP
    teacher_normed = rms_rows(teacher_rows, teacher_gain).reshape(N_DP, TOK_DEV, DT)
    student_normed = rms_rows(student_rows, student_gain).reshape(N_DP, TOK_DEV, DS)
    position = jnp.arange(TOK_DEV, dtype=jnp.int32) % LMAX
    owner_lengths = lengths.reshape(N_DP, SEQ_DEV)
    head_blocks = student_head.reshape(shards, VOC_DEV, DS).astype(jnp.float32)

    def group_step(head_total, inputs):
        teacher_block, student_block, seq_lengths = inputs
        live = (position < jnp.repeat(seq_lengths, LMAX, total_repeat_length=TOK_DEV)).astype(jnp.float32)
        teacher_logits = jnp.dot(teacher_block, teacher_head.T, preferred_element_type=jnp.float32)
        student_logits = jnp.dot(student_block, student_head.T, preferred_element_type=jnp.float32)
        teacher_lse = log_total(teacher_logits)
        student_lse = log_total(student_logits)
        teacher_prob = jnp.exp(teacher_logits - teacher_lse[:, None])
        student_prob = jnp.exp(student_logits - student_lse[:, None])
        logit_grad = (live[:, None] * (student_prob - teacher_prob)).astype(jnp.bfloat16)
        head_part = to_bfloat(jnp.dot(logit_grad.T, student_block, preferred_element_type=jnp.float32))
        grad_blocks = logit_grad.astype(jnp.float32).reshape(TOK_DEV, shards, VOC_DEV)
        row_parts = jnp.einsum('tnv,nvd->ntd', grad_blocks, head_blocks, precision=lax.Precision.HIGHEST)
        row_grad = lax.optimization_barrier(jnp.sum(to_bfloat(row_parts), axis=0))
        return (head_total + head_part, row_grad)
    head_grad, row_grad = lax.scan(group_step, jnp.zeros((VOCAB, DS), jnp.float32), (teacher_normed, student_normed, owner_lengths))
    row_grad = row_grad.reshape(TOKENS, DS)
    head_update = (head_grad * lax.rsqrt(jnp.mean(head_grad * head_grad) + epsilon)).astype(jnp.bfloat16)
    row_update = (row_grad * lax.rsqrt(jnp.mean(row_grad * row_grad) + epsilon)).astype(jnp.bfloat16)
    return (head_update, row_update)
```

```python
import functools

import jax
import jax.numpy as jnp
from jax import lax
from jax.experimental import pallas as pl
from jax.experimental.pallas import tpu as pltpu
from jax.sharding import PartitionSpec as P

DT = 5120
LMAX = 640


epsilon = 1e-06


def normalize(rows, gain):
    values = rows.astype(jnp.float32)
    mean_square = jnp.mean(values * values, axis=-1, keepdims=True)
    return (values * lax.rsqrt(mean_square + epsilon) * gain.astype(jnp.float32)).astype(
        jnp.bfloat16
    )


def against(rows, weights):
    return lax.dot_general(
        rows, weights, (((1,), (1,)), ((), ())), preferred_element_type=jnp.float32
    )


def body(
    teacher_rows, teacher_gain, teacher_head, student_rows, student_gain, student_head, lengths
):
    head_teacher, head_student = (
        lax.all_gather(teacher_head, "dp", axis=1, tiled=True),
        lax.all_gather(student_head, "dp", axis=1, tiled=True),
    )
    student_normed = normalize(student_rows, student_gain)
    tokens = student_rows.shape[0]
    values = teacher_rows.astype(jnp.float32)
    squares = lax.psum(jnp.sum(values * values, axis=1), ("group", "mp"))
    scale = lax.rsqrt(squares / DT + epsilon)
    teacher_normed = (values * scale[:, None] * teacher_gain.astype(jnp.float32)).astype(
        jnp.bfloat16
    )
    teacher_logits = against(
        lax.all_gather(teacher_normed, ("group", "mp"), axis=1, tiled=True), head_teacher
    )
    student_logits = against(student_normed, head_student)
    teacher_top, student_top = lax.pmax(
        (jnp.max(teacher_logits, axis=1), jnp.max(student_logits, axis=1)), ("group", "mp")
    )
    teacher_sum, student_sum = lax.psum(
        (
            jnp.sum(jnp.exp(teacher_logits - teacher_top[:, None]), axis=1),
            jnp.sum(jnp.exp(student_logits - student_top[:, None]), axis=1),
        ),
        ("group", "mp"),
    )
    teacher_lse = teacher_top + jnp.log(teacher_sum)
    student_lse = student_top + jnp.log(student_sum)
    position = jnp.arange(tokens, dtype=jnp.int32) % LMAX
    live = (position < jnp.repeat(lengths, LMAX, total_repeat_length=tokens)).astype(jnp.float32)
    teacher_prob = jnp.exp(teacher_logits - teacher_lse[:, None])
    student_prob = jnp.exp(student_logits - student_lse[:, None])
    logit_grad = (live[:, None] * (student_prob - teacher_prob)).astype(jnp.bfloat16)
    head_grad = (
        lax.psum_scatter(
            lax.dot_general(
                student_normed,
                logit_grad,
                (((0,), (0,)), ((), ())),
                preferred_element_type=jnp.float32,
            ).astype(jnp.bfloat16),
            "dp",
            scatter_dimension=0,
            tiled=True,
        )
        .astype(jnp.float32)
        .T
    )
    rows = lax.slice_in_dim(
        logit_grad,
        0,
        tokens // lax.axis_size(("group", "mp")) * lax.axis_size(("group", "mp")),
        axis=0,
    )
    row_grad = lax.psum_scatter(
        jnp.dot(rows, head_student, preferred_element_type=jnp.float32).astype(jnp.bfloat16),
        ("group", "mp"),
        scatter_dimension=0,
        tiled=True,
    ).astype(jnp.float32)
    devices = lax.axis_size(("dp", "group", "mp"))
    head_square, row_square = lax.psum(
        (jnp.sum(head_grad * head_grad), jnp.sum(row_grad * row_grad)), ("dp", "group", "mp")
    )
    head_update = head_grad * lax.rsqrt(head_square / (head_grad.size * devices) + epsilon)
    row_update = row_grad * lax.rsqrt(row_square / (row_grad.size * devices) + epsilon)
    return (head_update.astype(jnp.bfloat16), row_update.astype(jnp.bfloat16))


MESH = pl.DeviceIdType.MESH
COLS = 2
CHUNKS = 3


def dot_nt(a, b):
    return lax.dot_general(a, b, (((1,), (1,)), ((), ())), preferred_element_type=jnp.float32)


def step_kernel(
    n_dp,
    t_rows, t_gain, t_head, s_rows, s_gain, s_head, live,
    head_out, row_out,
    rows_all, gain_all, ht, hs, srow, sn, tn, t_exp, s_exp, lg_t, lg,
    stat, stat_in, hx_out, hx_in, hz_out, hz_in, h_acc,
    rc_out, rc_in, ry_out, ry_in, r_acc, sq, sq_in, sq2, sq2_in,
    send_sem, recv_sem, local_sem,
):
    n_z = n_dp // COLS
    d, g, m = lax.axis_index("dp"), lax.axis_index("group"), lax.axis_index("mp")
    z, x = d // COLS, d % COLS
    px, pg, pm = 1 - x, 1 - g, 1 - m
    me = 2 * g + m
    voc, tf = t_head.shape
    sf = s_head.shape[1]
    tok, ds = s_rows.shape
    blocks = 4
    own = tok // blocks
    peers = [dict(group=g, mp=pm), dict(group=pg, mp=m), dict(group=pg, mp=pm)]
    peers_gm = [2 * g + pm, 2 * pg + m, 2 * pg + pm]

    barrier = pltpu.get_barrier_semaphore()
    for peer in peers:
        pl.semaphore_signal(barrier, inc=1, device_id=peer, device_id_type=MESH)
    for k in range(1, n_dp):
        pl.semaphore_signal(
            barrier, inc=1, device_id={"dp": (d + k) % n_dp}, device_id_type=MESH
        )

    locals_ = [
        pltpu.make_async_copy(src, dst, local_sem.at[i])
        for i, (src, dst) in enumerate(
            [
                (s_rows, srow),
                (t_rows, rows_all.at[me]),
                (t_head, ht.at[d]),
                (s_head, hs.at[d]),
                (t_gain, gain_all.at[me]),
            ]
        )
    ]
    for copy in locals_:
        copy.start()
    pl.semaphore_wait(barrier, 3 + n_dp - 1)

    sent = []

    def send(src, dst, to):
        i = len(sent)
        copy = pltpu.make_async_remote_copy(
            src_ref=src, dst_ref=dst, send_sem=send_sem.at[i], recv_sem=recv_sem.at[i],
            device_id=to, device_id_type=MESH,
        )
        copy.start()
        sent.append(copy)
        return i

    def arrive(i, dst):
        pltpu.make_async_remote_copy(
            src_ref=dst, dst_ref=dst, send_sem=send_sem.at[i], recv_sem=recv_sem.at[i],
            device_id={"dp": d}, device_id_type=MESH,
        ).wait_recv()

    def col(k):
        return ((z + k) % n_z) * COLS + x

    to_x = {"dp": z * COLS + px}
    to_y = {"mp": pm}
    to_core = {"group": pg}
    piece = voc // CHUNKS

    def part(ref, c):
        return ref.at[pl.ds(c * piece, piece), :]

    s_z = {k: send(s_head, hs.at[d], {"dp": col(k)}) for k in range(1, n_z)}
    s_x = {0: send(s_head, hs.at[d], to_x)}
    rows_y = send(t_rows, rows_all.at[me], to_y)
    t_z, t_x = {}, {}
    for c in range(CHUNKS):
        for k in range(1, n_z):
            t_z[c, k] = send(part(t_head, c), part(ht.at[d], c), {"dp": col(k)})
        t_x[c, 0] = send(part(t_head, c), part(ht.at[d], c), to_x)
    rows_core = send(t_rows, rows_all.at[me], to_core)
    gains = [send(t_gain, gain_all.at[me], peer) for peer in peers]

    locals_[0].wait()
    tile = 32

    def student_tile(i, _):
        at = pl.ds(pl.multiple_of(i * tile, tile), tile)
        values = srow[at, :].astype(jnp.float32)
        mean_square = jnp.mean(values * values, axis=-1, keepdims=True)
        sn[at, :] = (values * lax.rsqrt(mean_square + epsilon) * s_gain[...]).astype(jnp.bfloat16)
        return 0

    lax.fori_loop(0, tok // tile, student_tile, 0)

    for k in range(1, n_z):
        slot = hs.at[col(n_z - k)]
        arrive(s_z[k], slot)
        s_x[k] = send(slot, slot, to_x)

    def forward(c, k):
        slot = part(ht.at[col(n_z - k)], c)
        arrive(t_z[c, k], slot)
        t_x[c, k] = send(slot, slot, to_x)

    for k in range(1, n_z):
        forward(0, k)
    locals_[3].wait()
    for k in range(n_z):
        arrive(s_x[k], hs.at[((z + n_z - k) % n_z) * COLS + px])

    def student_block(f, _):
        at = pl.ds(pl.multiple_of(f * sf, sf), sf)
        s_exp[...] += dot_nt(hs[f], sn[:, at])
        return 0

    s_exp[...] = jnp.zeros_like(s_exp)
    lax.fori_loop(0, n_dp, student_block, 0)
    for k in range(1, n_z):
        forward(1, k)

    def softmax_part(ref, row):
        values = ref[...]
        top = jnp.max(values, axis=0, keepdims=True)
        exps = jnp.exp(values - top)
        ref[...] = exps
        stat[row : row + 1, :] = top
        stat[row + 1 : row + 2, :] = jnp.sum(exps, axis=0, keepdims=True)

    stat[...] = jnp.zeros_like(stat)
    softmax_part(s_exp, 0)

    arrive(rows_y, rows_all.at[peers_gm[0]])
    rows_far = send(rows_all.at[peers_gm[0]], rows_all.at[peers_gm[0]], to_core)
    for k in range(1, n_z):
        forward(2, k)
    locals_[1].wait()
    locals_[4].wait()
    for i in range(3):
        arrive(gains[i], gain_all.at[peers_gm[i]])
    arrive(rows_core, rows_all.at[peers_gm[1]])
    arrive(rows_far, rows_all.at[peers_gm[2]])
    width = t_rows.shape[1]

    def teacher_tile(i, _):
        at = pl.ds(pl.multiple_of(i * tile, tile), tile)
        total = jnp.zeros((tile, 1), jnp.float32)
        for j in range(blocks):
            values = rows_all[j, at, :].astype(jnp.float32)
            total += jnp.sum(values * values, axis=-1, keepdims=True)
        scale = lax.rsqrt(total / (blocks * width) + epsilon)
        for j in range(blocks):
            values = rows_all[j, at, :].astype(jnp.float32)
            tn[j, at, :] = (values * scale * gain_all[j, 0:1, :]).astype(jnp.bfloat16)
        return 0

    lax.fori_loop(0, tok // tile, teacher_tile, 0)

    per = width // tf

    def teacher_block(f):
        at = pl.ds(pl.multiple_of((f % per) * tf, tf), tf)
        t_exp[...] += dot_nt(ht[f], tn[f // per, :, at])

    locals_[2].wait()
    t_exp[...] = jnp.zeros_like(t_exp)

    def own_column(i, _):
        teacher_block(i * COLS + x)
        return 0

    lax.fori_loop(0, n_z, own_column, 0)
    for k in range(n_z):
        f = ((z + n_z - k) % n_z) * COLS + px
        for c in range(CHUNKS):
            arrive(t_x[c, k], part(ht.at[f], c))

    def other_column(i, _):
        teacher_block(i * COLS + px)
        return 0

    lax.fori_loop(0, n_z, other_column, 0)
    softmax_part(t_exp, 2)

    stats = [send(stat, stat_in.at[i], peers[i]) for i in range(3)]
    for i in range(3):
        arrive(stats[i], stat_in.at[i])

    def factor(row):
        tops = [stat[row : row + 1, :]] + [stat_in[i, row : row + 1, :] for i in range(3)]
        sums = [stat[row + 1 : row + 2, :]] + [
            stat_in[i, row + 1 : row + 2, :] for i in range(3)
        ]
        top = functools.reduce(jnp.maximum, tops)
        total = sum(s * jnp.exp(t - top) for s, t in zip(sums, tops))
        return live[0:1, :] * jnp.exp(tops[0] - top - jnp.log(total))

    grad = s_exp[...] * factor(0) - t_exp[...] * factor(2)
    lg_t[...] = grad.astype(jnp.bfloat16)
    lg[...] = grad.T.astype(jnp.bfloat16)

    def head_block(f):
        at = pl.ds(pl.multiple_of(f * sf, sf), sf)
        return jnp.dot(lg_t[...], sn[:, at], preferred_element_type=jnp.float32)

    order = [*range(1, n_z), 0]
    hx, hz = {}, {}
    for k in order:
        hx_out[k] = head_block(((z + k) % n_z) * COLS + px).astype(jnp.bfloat16)
        hx[k] = send(hx_out.at[k], hx_in.at[k], to_x)

    def row_block(t, dst, taken=None):
        at = pl.ds(pl.multiple_of(t * own, own), own)

        def step(f, _):
            to = pl.ds(pl.multiple_of(f * sf, sf), sf)
            value = jnp.dot(lg[at, :], hs[f], preferred_element_type=jnp.float32)
            if taken is not None:
                value += taken[:, to].astype(jnp.float32)
            dst[:, to] = value.astype(dst.dtype)
            return 0

        lax.fori_loop(0, n_dp, step, 0)

    rc = []
    for i, mp in enumerate((pm, m)):
        row_block(2 * pg + mp, rc_out.at[i])
        rc.append(send(rc_out.at[i], rc_in.at[i], to_core))

    for k in order[:-1]:
        value = head_block(col(k))
        arrive(hx[k], hx_in.at[k])
        hz_out[k - 1] = (value + hx_in[k].astype(jnp.float32)).astype(jnp.bfloat16)
        hz[k] = send(hz_out.at[k - 1], hz_in.at[k - 1], {"dp": col(k)})

    arrive(rc[0], rc_in.at[0])
    row_block(2 * g + pm, ry_out, rc_in.at[0])
    ry = send(ry_out, ry_in, to_y)
    value = head_block(d)
    arrive(hx[0], hx_in.at[0])
    h_acc[...] = value + hx_in[0].astype(jnp.float32)
    arrive(rc[1], rc_in.at[1])
    row_block(2 * g + m, r_acc, rc_in.at[1])
    for k in range(1, n_z):
        arrive(hz[k], hz_in.at[k - 1])
    total = h_acc[...] + sum(hz_in[k].astype(jnp.float32) for k in range(n_z - 1))
    h_acc[...] = total

    def fold(values):
        lanes = jnp.sum(values * values, axis=0, keepdims=True)
        return sum(lanes[:, i : i + 128] for i in range(0, lanes.shape[1], 128))

    sq[...] = jnp.zeros_like(sq)
    sq[0:1, :] = fold(total)
    arrive(ry, ry_in)

    def row_sum(i, acc):
        at = pl.ds(pl.multiple_of(i * tile, tile), tile)
        values = r_acc[at, :] + ry_in[at, :].astype(jnp.float32)
        r_acc[at, :] = values
        return acc + fold(values)

    sq[1:2, :] = lax.fori_loop(0, own // tile, row_sum, jnp.zeros((1, 128), jnp.float32))

    first = [send(sq, sq_in.at[i], peers[i]) for i in range(3)]
    for i in range(3):
        arrive(first[i], sq_in.at[i])
    sq2[...] = sq[...] + sq_in[0] + sq_in[1] + sq_in[2]
    second = [send(sq2, sq2_in.at[k - 1], {"dp": (d + k) % n_dp}) for k in range(1, n_dp)]
    for k in range(1, n_dp):
        arrive(second[k - 1], sq2_in.at[k - 1])
    squares = jnp.sum(sq2[...] + jnp.sum(sq2_in[...], axis=0), axis=1, keepdims=True)
    devices = n_dp * blocks
    head_out[...] = (
        h_acc[...] * lax.rsqrt(squares[0:1, :] / (voc * sf * devices) + epsilon)
    ).astype(jnp.bfloat16)
    row_out[...] = (
        r_acc[...] * lax.rsqrt(squares[1:2, :] / (own * ds * devices) + epsilon)
    ).astype(jnp.bfloat16)
    for copy in sent:
        copy.wait_send()


def fused(
    teacher_rows, teacher_gain, teacher_head, student_rows, student_gain, student_head, lengths
):
    n_dp = lax.axis_size("dp")
    tok, width = teacher_rows.shape
    voc, tf = teacher_head.shape
    ds, sf = student_rows.shape[1], student_head.shape[1]
    n_z, own = n_dp // COLS, tok // 4
    position = jnp.arange(tok, dtype=jnp.int32) % LMAX
    live = (position < jnp.repeat(lengths, LMAX, total_repeat_length=tok)).astype(jnp.float32)
    bf, f32 = jnp.bfloat16, jnp.float32
    copies = 3 + 2 * n_z - 1 + CHUNKS * (2 * n_z - 1) + 3 + 3 + 2 * n_z - 1 + 3 + 3 + n_dp - 1
    anywhere, vmem = pl.BlockSpec(memory_space=pl.ANY), pl.BlockSpec(memory_space=pltpu.VMEM)
    return pl.pallas_call(
        functools.partial(step_kernel, n_dp),
        out_shape=(
            jax.ShapeDtypeStruct((voc, sf), bf),
            jax.ShapeDtypeStruct((own, ds), bf),
        ),
        in_specs=[anywhere, anywhere, anywhere, anywhere, vmem, anywhere, vmem],
        out_specs=(vmem, vmem),
        scratch_shapes=[
            pltpu.VMEM((4, tok, width), bf),
            pltpu.VMEM((4, 8, width), f32),
            pltpu.VMEM((n_dp, voc, tf), bf),
            pltpu.VMEM((n_dp, voc, sf), bf),
            pltpu.VMEM((tok, ds), bf),
            pltpu.VMEM((tok, ds), bf),
            pltpu.VMEM((4, tok, width), bf),
            pltpu.VMEM((voc, tok), f32),
            pltpu.VMEM((voc, tok), f32),
            pltpu.VMEM((voc, tok), bf),
            pltpu.VMEM((tok, voc), bf),
            pltpu.VMEM((8, tok), f32),
            pltpu.VMEM((3, 8, tok), f32),
            pltpu.VMEM((n_z, voc, sf), bf),
            pltpu.VMEM((n_z, voc, sf), bf),
            pltpu.VMEM((n_z - 1, voc, sf), bf),
            pltpu.VMEM((n_z - 1, voc, sf), bf),
            pltpu.VMEM((voc, sf), f32),
            pltpu.VMEM((2, own, ds), bf),
            pltpu.VMEM((2, own, ds), bf),
            pltpu.VMEM((own, ds), bf),
            pltpu.VMEM((own, ds), bf),
            pltpu.VMEM((own, ds), f32),
            pltpu.VMEM((8, 128), f32),
            pltpu.VMEM((3, 8, 128), f32),
            pltpu.VMEM((8, 128), f32),
            pltpu.VMEM((n_dp - 1, 8, 128), f32),
            pltpu.SemaphoreType.DMA((copies,)),
            pltpu.SemaphoreType.DMA((copies,)),
            pltpu.SemaphoreType.DMA((5,)),
        ],
        compiler_params=pltpu.CompilerParams(
            collective_id=0, has_side_effects=True, vmem_limit_bytes=56 << 20
        ),
    )(
        teacher_rows,
        jnp.broadcast_to(teacher_gain.astype(f32), (8, width)),
        teacher_head,
        student_rows,
        student_gain.astype(f32)[None, :],
        student_head,
        jnp.broadcast_to(live, (8, tok)),
    )


def step(*args):
    t_rows, _, t_head, s_rows, _, s_head, _ = args
    fits = (
        (lax.axis_size("group"), lax.axis_size("mp"), lax.axis_size("dp") % COLS) == (2, 2, 0)
        and lax.axis_size("dp") <= 16
        and t_head.shape[1] % 128 == 0
        and s_head.shape[1] % 128 == 0
        and t_rows.shape[1] % t_head.shape[1] == 0
        and t_head.shape[0] % (16 * CHUNKS) == 0
        and s_rows.shape[0] % 128 == 0
    )
    return fused(*args) if fits else body(*args)


def solution(mesh):
    placed = (
        P("dp", ("group", "mp")),
        P(("group", "mp")),
        P(("group", "mp"), "dp"),
        P("dp", None),
        P(),
        P(("group", "mp"), "dp"),
        P("dp"),
    )
    return jax.shard_map(
        step,
        mesh=mesh,
        in_specs=placed,
        out_specs=(P(("group", "mp"), "dp"), P(("dp", "group", "mp"), None)),
        check_vma=False,
    )
```

```python
import functools

import jax
import jax.numpy as jnp
from jax import lax
from jax.experimental import pallas as pl
from jax.experimental.pallas import tpu as pltpu
from jax.sharding import PartitionSpec as P

DT = 5120
LMAX = 640


epsilon = 1e-06


def normalize(rows, gain):
    values = rows.astype(jnp.float32)
    mean_square = jnp.mean(values * values, axis=-1, keepdims=True)
    return (values * lax.rsqrt(mean_square + epsilon) * gain.astype(jnp.float32)).astype(
        jnp.bfloat16
    )


def against(rows, weights):
    return lax.dot_general(
        rows, weights, (((1,), (1,)), ((), ())), preferred_element_type=jnp.float32
    )


def body(
    teacher_rows, teacher_gain, teacher_head, student_rows, student_gain, student_head, lengths
):
    head_teacher, head_student = (
        lax.all_gather(teacher_head, "dp", axis=1, tiled=True),
        lax.all_gather(student_head, "dp", axis=1, tiled=True),
    )
    student_normed = normalize(student_rows, student_gain)
    tokens = student_rows.shape[0]
    values = teacher_rows.astype(jnp.float32)
    squares = lax.psum(jnp.sum(values * values, axis=1), ("group", "mp"))
    scale = lax.rsqrt(squares / DT + epsilon)
    teacher_normed = (values * scale[:, None] * teacher_gain.astype(jnp.float32)).astype(
        jnp.bfloat16
    )
    teacher_logits = against(
        lax.all_gather(teacher_normed, ("group", "mp"), axis=1, tiled=True), head_teacher
    )
    student_logits = against(student_normed, head_student)
    teacher_top, student_top = lax.pmax(
        (jnp.max(teacher_logits, axis=1), jnp.max(student_logits, axis=1)), ("group", "mp")
    )
    teacher_sum, student_sum = lax.psum(
        (
            jnp.sum(jnp.exp(teacher_logits - teacher_top[:, None]), axis=1),
            jnp.sum(jnp.exp(student_logits - student_top[:, None]), axis=1),
        ),
        ("group", "mp"),
    )
    teacher_lse = teacher_top + jnp.log(teacher_sum)
    student_lse = student_top + jnp.log(student_sum)
    position = jnp.arange(tokens, dtype=jnp.int32) % LMAX
    live = (position < jnp.repeat(lengths, LMAX, total_repeat_length=tokens)).astype(jnp.float32)
    teacher_prob = jnp.exp(teacher_logits - teacher_lse[:, None])
    student_prob = jnp.exp(student_logits - student_lse[:, None])
    logit_grad = (live[:, None] * (student_prob - teacher_prob)).astype(jnp.bfloat16)
    head_grad = (
        lax.psum_scatter(
            lax.dot_general(
                student_normed,
                logit_grad,
                (((0,), (0,)), ((), ())),
                preferred_element_type=jnp.float32,
            ).astype(jnp.bfloat16),
            "dp",
            scatter_dimension=0,
            tiled=True,
        )
        .astype(jnp.float32)
        .T
    )
    rows = lax.slice_in_dim(
        logit_grad,
        0,
        tokens // lax.axis_size(("group", "mp")) * lax.axis_size(("group", "mp")),
        axis=0,
    )
    row_grad = lax.psum_scatter(
        jnp.dot(rows, head_student, preferred_element_type=jnp.float32).astype(jnp.bfloat16),
        ("group", "mp"),
        scatter_dimension=0,
        tiled=True,
    ).astype(jnp.float32)
    devices = lax.axis_size(("dp", "group", "mp"))
    head_square, row_square = lax.psum(
        (jnp.sum(head_grad * head_grad), jnp.sum(row_grad * row_grad)), ("dp", "group", "mp")
    )
    head_update = head_grad * lax.rsqrt(head_square / (head_grad.size * devices) + epsilon)
    row_update = row_grad * lax.rsqrt(row_square / (row_grad.size * devices) + epsilon)
    return (head_update.astype(jnp.bfloat16), row_update.astype(jnp.bfloat16))


MESH = pl.DeviceIdType.MESH
COLS = 2
CHUNKS = 3


def dot_nt(a, b):
    return lax.dot_general(a, b, (((1,), (1,)), ((), ())), preferred_element_type=jnp.float32)


def step_kernel(
    n_dp,
    t_rows, t_gain, t_head, s_rows, s_gain, s_head, lengths,
    head_out, row_out,
    rows_all, gain_all, ht, hs, srow, sn, tn, t_exp, s_exp, lg_t, lg,
    stat, stat_in, hx_out, hx_in, hz_out, hz_in, h_acc,
    rc_out, rc_in, ry_out, ry_in, r_acc, sq, sq_in, sq2, sq2_in,
    send_sem, recv_sem, local_sem,
):
    n_z = n_dp // COLS
    d, g, m = lax.axis_index("dp"), lax.axis_index("group"), lax.axis_index("mp")
    z, x = d // COLS, d % COLS
    px, pg, pm = 1 - x, 1 - g, 1 - m
    me = 2 * g + m
    voc, tf = t_head.shape
    sf = s_head.shape[1]
    tok, ds = s_rows.shape
    blocks = 4
    own = tok // blocks
    peers = [dict(group=g, mp=pm), dict(group=pg, mp=m), dict(group=pg, mp=pm)]
    peers_gm = [2 * g + pm, 2 * pg + m, 2 * pg + pm]

    barrier = pltpu.get_barrier_semaphore()
    for peer in peers:
        pl.semaphore_signal(barrier, inc=1, device_id=peer, device_id_type=MESH)
    for k in range(1, n_dp):
        pl.semaphore_signal(
            barrier, inc=1, device_id={"dp": (d + k) % n_dp}, device_id_type=MESH
        )

    locals_ = [
        pltpu.make_async_copy(src, dst, local_sem.at[i])
        for i, (src, dst) in enumerate(
            [
                (s_rows, srow),
                (t_rows, rows_all.at[me]),
                (t_head, ht.at[d]),
                (s_head, hs.at[d]),
            ]
        )
    ]
    for copy in locals_:
        copy.start()
    gain_all[me] = jnp.broadcast_to(
        t_gain[...].astype(jnp.float32).reshape(1, -1), gain_all.shape[1:]
    )
    pl.semaphore_wait(barrier, 3 + n_dp - 1)

    sent, always = [], None

    def send(src, dst, to, when=always):
        i = len(sent)
        copy = pltpu.make_async_remote_copy(
            src_ref=src, dst_ref=dst, send_sem=send_sem.at[i], recv_sem=recv_sem.at[i],
            device_id=to, device_id_type=MESH,
        )
        if when is None:
            copy.start()
        else:
            pl.when(when)(copy.start)
        sent.append((copy, when))
        return i

    def arrive(i, dst):
        pltpu.make_async_remote_copy(
            src_ref=dst, dst_ref=dst, send_sem=send_sem.at[i], recv_sem=recv_sem.at[i],
            device_id={"dp": d}, device_id_type=MESH,
        ).wait_recv()

    def col(k):
        return ((z + k) % n_z) * COLS + x

    to_x = {"dp": z * COLS + px}
    to_y = {"mp": pm}
    to_core = {"group": pg}
    piece = voc // CHUNKS

    def part(ref, c):
        return ref.at[pl.ds(c * piece, piece), :]

    parts = [(s_head, hs, None)] + [(t_head, ht, c) for c in range(CHUNKS)]
    ways = (1, -1)

    def view(ref, c):
        return ref if c is None else part(ref, c)

    def inside(at):
        return (at >= 0) & (at < n_z)

    along, across = {}, {}
    for p, (src, dst, c) in enumerate(parts):
        for way in ways:
            along[way, 0, p] = send(
                view(src, c), view(dst.at[d], c), {"dp": (z + way) % n_z * COLS + x},
                inside(z + way),
            )
        across[p] = send(view(src, c), view(dst.at[d], c), to_x)
        if p == 0:
            rows_y = send(t_rows, rows_all.at[me], to_y)
    rows_core = send(t_rows, rows_all.at[me], to_core)
    gains = [send(gain_all.at[me], gain_all.at[me], peer) for peer in peers]

    def origin(way, hop):
        return z - way * (hop + 1)

    def block(way, hop, column):
        return (origin(way, hop) + n_z) % n_z * COLS + column

    def forward(hop, p):
        _, dst, c = parts[p]
        for way in ways:
            here = inside(origin(way, hop))
            slot = view(dst.at[block(way, hop, x)], c)

            @pl.when(here)
            def _():
                arrive(along[way, hop, p], slot)

            if hop < n_z - 2:
                along[way, hop + 1, p] = send(
                    slot, slot, {"dp": (z + way + n_z) % n_z * COLS + x}, here & inside(z + way)
                )
            across[way, hop, p] = send(slot, slot, to_x, here)

    locals_[0].wait()
    tile = 32

    gain = s_gain[...].astype(jnp.float32).reshape(1, -1)

    def student_tile(i, _):
        at = pl.ds(pl.multiple_of(i * tile, tile), tile)
        values = srow[at, :].astype(jnp.float32)
        mean_square = jnp.mean(values * values, axis=-1, keepdims=True)
        sn[at, :] = (values * lax.rsqrt(mean_square + epsilon) * gain).astype(jnp.bfloat16)
        return 0

    lax.fori_loop(0, tok // tile, student_tile, 0)

    for hop in range(n_z - 1):
        for p in range(len(parts)):
            forward(hop, p)
        if hop == n_z - 3:
            arrive(rows_y, rows_all.at[peers_gm[0]])
            rows_far = send(rows_all.at[peers_gm[0]], rows_all.at[peers_gm[0]], to_core)

    locals_[3].wait()
    arrive(across[0], hs.at[z * COLS + px])
    for hop in range(n_z - 1):
        for way in ways:

            @pl.when(inside(origin(way, hop)))
            def _():
                arrive(across[way, hop, 0], hs.at[block(way, hop, px)])

    def student_block(f, _):
        at = pl.ds(pl.multiple_of(f * sf, sf), sf)
        s_exp[...] += dot_nt(hs[f], sn[:, at])
        return 0

    s_exp[...] = jnp.zeros_like(s_exp)
    lax.fori_loop(0, n_dp, student_block, 0)

    def softmax_part(ref, row):
        values = ref[...]
        top = jnp.max(values, axis=0, keepdims=True)
        exps = jnp.exp(values - top)
        ref[...] = exps
        stat[row : row + 1, :] = top
        stat[row + 1 : row + 2, :] = jnp.sum(exps, axis=0, keepdims=True)

    stat[...] = jnp.zeros_like(stat)
    softmax_part(s_exp, 0)

    locals_[1].wait()
    for i in range(3):
        arrive(gains[i], gain_all.at[peers_gm[i]])
    arrive(rows_core, rows_all.at[peers_gm[1]])
    arrive(rows_far, rows_all.at[peers_gm[2]])
    width = t_rows.shape[1]

    def teacher_tile(i, _):
        at = pl.ds(pl.multiple_of(i * tile, tile), tile)
        total = jnp.zeros((tile, 1), jnp.float32)
        for j in range(blocks):
            values = rows_all[j, at, :].astype(jnp.float32)
            total += jnp.sum(values * values, axis=-1, keepdims=True)
        scale = lax.rsqrt(total / (blocks * width) + epsilon)
        for j in range(blocks):
            values = rows_all[j, at, :].astype(jnp.float32)
            tn[j, at, :] = (values * scale * gain_all[j, 0:1, :]).astype(jnp.bfloat16)
        return 0

    lax.fori_loop(0, tok // tile, teacher_tile, 0)

    per = width // tf

    def teacher_block(f):
        at = pl.ds(pl.multiple_of((f % per) * tf, tf), tf)
        t_exp[...] += dot_nt(ht[f], tn[f // per, :, at])

    locals_[2].wait()
    t_exp[...] = jnp.zeros_like(t_exp)

    def own_column(i, _):
        teacher_block(i * COLS + x)
        return 0

    lax.fori_loop(0, n_z, own_column, 0)
    for p in range(1, len(parts)):
        arrive(across[p], part(ht.at[z * COLS + px], parts[p][2]))
    teacher_block(z * COLS + px)
    for hop in range(n_z - 1):
        for way in ways:

            @pl.when(inside(origin(way, hop)))
            def _():
                f = block(way, hop, px)
                for p in range(1, len(parts)):
                    arrive(across[way, hop, p], part(ht.at[f], parts[p][2]))
                teacher_block(f)

    softmax_part(t_exp, 2)

    stats = [send(stat, stat_in.at[i], peers[i]) for i in range(3)]
    for i in range(3):
        arrive(stats[i], stat_in.at[i])

    position = lax.broadcasted_iota(jnp.int32, (1, tok), 1) % LMAX
    live = (position < lengths[0]).astype(jnp.float32)

    def factor(row):
        tops = [stat[row : row + 1, :]] + [stat_in[i, row : row + 1, :] for i in range(3)]
        sums = [stat[row + 1 : row + 2, :]] + [
            stat_in[i, row + 1 : row + 2, :] for i in range(3)
        ]
        top = functools.reduce(jnp.maximum, tops)
        total = sum(s * jnp.exp(t - top) for s, t in zip(sums, tops))
        return live * jnp.exp(tops[0] - top - jnp.log(total))

    grad = s_exp[...] * factor(0) - t_exp[...] * factor(2)
    lg_t[...] = grad.astype(jnp.bfloat16)
    lg[...] = grad.T.astype(jnp.bfloat16)

    def head_block(f):
        at = pl.ds(pl.multiple_of(f * sf, sf), sf)
        return jnp.dot(lg_t[...], sn[:, at], preferred_element_type=jnp.float32)

    def row_block(t, dst, taken=None):
        at = pl.ds(pl.multiple_of(t * own, own), own)

        def step(f, _):
            to = pl.ds(pl.multiple_of(f * sf, sf), sf)
            value = jnp.dot(lg[at, :], hs[f], preferred_element_type=jnp.float32)
            if taken is not None:
                value += taken[:, to].astype(jnp.float32)
            dst[:, to] = value.astype(dst.dtype)
            return 0

        lax.fori_loop(0, n_dp, step, 0)

    def to_mate(i, mp):
        row_block(2 * pg + mp, rc_out.at[i])
        return send(rc_out.at[i], rc_in.at[i], to_core)

    order = [*range(1, n_z), 0]
    hx, hz = {}, {}
    rc = [to_mate(0, pm)]
    for k in order:
        hx_out[k] = head_block(((z + k) % n_z) * COLS + px).astype(jnp.bfloat16)
        hx[k] = send(hx_out.at[k], hx_in.at[k], to_x)
    rc.append(to_mate(1, m))
    arrive(rc[0], rc_in.at[0])
    row_block(2 * g + pm, ry_out, rc_in.at[0])
    ry = send(ry_out, ry_in, to_y)
    for k in order[:-1]:
        value = head_block(col(k))
        arrive(hx[k], hx_in.at[k])
        hz_out[k - 1] = (value + hx_in[k].astype(jnp.float32)).astype(jnp.bfloat16)
        hz[k] = send(hz_out.at[k - 1], hz_in.at[k - 1], {"dp": col(k)})
    value = head_block(d)
    arrive(hx[0], hx_in.at[0])
    h_acc[...] = value + hx_in[0].astype(jnp.float32)
    arrive(rc[1], rc_in.at[1])
    row_block(2 * g + m, r_acc, rc_in.at[1])
    for k in range(1, n_z):
        arrive(hz[k], hz_in.at[k - 1])
    total = h_acc[...] + sum(hz_in[k].astype(jnp.float32) for k in range(n_z - 1))
    h_acc[...] = total

    def fold(values):
        lanes = jnp.sum(values * values, axis=0, keepdims=True)
        return sum(lanes[:, i : i + 128] for i in range(0, lanes.shape[1], 128))

    sq[...] = jnp.zeros_like(sq)
    sq[0:1, :] = fold(total)
    arrive(ry, ry_in)

    def row_sum(i, acc):
        at = pl.ds(pl.multiple_of(i * tile, tile), tile)
        values = r_acc[at, :] + ry_in[at, :].astype(jnp.float32)
        r_acc[at, :] = values
        return acc + fold(values)

    sq[1:2, :] = lax.fori_loop(0, own // tile, row_sum, jnp.zeros((1, 128), jnp.float32))

    first = [send(sq, sq_in.at[i], peers[i]) for i in range(3)]
    for i in range(3):
        arrive(first[i], sq_in.at[i])
    sq2[...] = sq[...] + sq_in[0] + sq_in[1] + sq_in[2]
    second = [send(sq2, sq2_in.at[k - 1], {"dp": (d + k) % n_dp}) for k in range(1, n_dp)]
    for k in range(1, n_dp):
        arrive(second[k - 1], sq2_in.at[k - 1])
    squares = jnp.sum(sq2[...] + jnp.sum(sq2_in[...], axis=0), axis=1, keepdims=True)
    devices = n_dp * blocks
    head_out[...] = (
        h_acc[...] * lax.rsqrt(squares[0:1, :] / (voc * sf * devices) + epsilon)
    ).astype(jnp.bfloat16)
    row_out[...] = (
        r_acc[...] * lax.rsqrt(squares[1:2, :] / (own * ds * devices) + epsilon)
    ).astype(jnp.bfloat16)
    for copy, when in sent:
        if when is None:
            copy.wait_send()
        else:
            pl.when(when)(copy.wait_send)


def fused(
    teacher_rows, teacher_gain, teacher_head, student_rows, student_gain, student_head, lengths
):
    n_dp = lax.axis_size("dp")
    tok, width = teacher_rows.shape
    voc, tf = teacher_head.shape
    ds, sf = student_rows.shape[1], student_head.shape[1]
    n_z, own = n_dp // COLS, tok // 4
    bf, f32 = jnp.bfloat16, jnp.float32
    hops = (1 + CHUNKS) * (n_z - 1) * 4 + (1 + CHUNKS)
    copies = 3 + hops + 3 + 3 + 2 * n_z - 1 + 3 + 3 + n_dp - 1
    anywhere, vmem = pl.BlockSpec(memory_space=pl.ANY), pl.BlockSpec(memory_space=pltpu.VMEM)
    scalars = pl.BlockSpec(memory_space=pltpu.SMEM)
    return pl.pallas_call(
        functools.partial(step_kernel, n_dp),
        out_shape=(
            jax.ShapeDtypeStruct((voc, sf), bf),
            jax.ShapeDtypeStruct((own, ds), bf),
        ),
        in_specs=[anywhere, vmem, anywhere, anywhere, vmem, anywhere, scalars],
        out_specs=(vmem, vmem),
        scratch_shapes=[
            pltpu.VMEM((4, tok, width), bf),
            pltpu.VMEM((4, 8, width), f32),
            pltpu.VMEM((n_dp, voc, tf), bf),
            pltpu.VMEM((n_dp, voc, sf), bf),
            pltpu.VMEM((tok, ds), bf),
            pltpu.VMEM((tok, ds), bf),
            pltpu.VMEM((4, tok, width), bf),
            pltpu.VMEM((voc, tok), f32),
            pltpu.VMEM((voc, tok), f32),
            pltpu.VMEM((voc, tok), bf),
            pltpu.VMEM((tok, voc), bf),
            pltpu.VMEM((8, tok), f32),
            pltpu.VMEM((3, 8, tok), f32),
            pltpu.VMEM((n_z, voc, sf), bf),
            pltpu.VMEM((n_z, voc, sf), bf),
            pltpu.VMEM((n_z - 1, voc, sf), bf),
            pltpu.VMEM((n_z - 1, voc, sf), bf),
            pltpu.VMEM((voc, sf), f32),
            pltpu.VMEM((2, own, ds), bf),
            pltpu.VMEM((2, own, ds), bf),
            pltpu.VMEM((own, ds), bf),
            pltpu.VMEM((own, ds), bf),
            pltpu.VMEM((own, ds), f32),
            pltpu.VMEM((8, 128), f32),
            pltpu.VMEM((3, 8, 128), f32),
            pltpu.VMEM((8, 128), f32),
            pltpu.VMEM((n_dp - 1, 8, 128), f32),
            pltpu.SemaphoreType.DMA((copies,)),
            pltpu.SemaphoreType.DMA((copies,)),
            pltpu.SemaphoreType.DMA((4,)),
        ],
        compiler_params=pltpu.CompilerParams(
            collective_id=0, has_side_effects=True, vmem_limit_bytes=56 << 20
        ),
    )(
        teacher_rows,
        teacher_gain,
        teacher_head,
        student_rows,
        student_gain,
        student_head,
        lengths,
    )


def step(*args):
    t_rows, _, t_head, s_rows, _, s_head, lengths = args
    fits = (
        (lax.axis_size("group"), lax.axis_size("mp"), lax.axis_size("dp") % COLS) == (2, 2, 0)
        and lax.axis_size("dp") <= 16
        and t_head.shape[1] % 128 == 0
        and s_head.shape[1] % 128 == 0
        and t_rows.shape[1] % t_head.shape[1] == 0
        and t_head.shape[0] % (16 * CHUNKS) == 0
        and s_rows.shape[0] % 128 == 0
        and lengths.shape[0] == 1
    )
    return fused(*args) if fits else body(*args)


def solution(mesh):
    placed = (
        P("dp", ("group", "mp")),
        P(("group", "mp")),
        P(("group", "mp"), "dp"),
        P("dp", None),
        P(),
        P(("group", "mp"), "dp"),
        P("dp"),
    )
    return jax.shard_map(
        step,
        mesh=mesh,
        in_specs=placed,
        out_specs=(P(("group", "mp"), "dp"), P(("dp", "group", "mp"), None)),
        check_vma=False,
    )
```

```python
import functools

import jax
import jax.numpy as jnp
from jax import lax
from jax.experimental import pallas as pl
from jax.experimental.pallas import tpu as pltpu
from jax.sharding import PartitionSpec as P

DT = 5120
LMAX = 640


epsilon = 1e-06


def normalize(rows, gain):
    values = rows.astype(jnp.float32)
    mean_square = jnp.mean(values * values, axis=-1, keepdims=True)
    return (values * lax.rsqrt(mean_square + epsilon) * gain.astype(jnp.float32)).astype(
        jnp.bfloat16
    )


def against(rows, weights):
    return lax.dot_general(
        rows, weights, (((1,), (1,)), ((), ())), preferred_element_type=jnp.float32
    )


def body(
    teacher_rows, teacher_gain, teacher_head, student_rows, student_gain, student_head, lengths
):
    head_teacher, head_student = (
        lax.all_gather(teacher_head, "dp", axis=1, tiled=True),
        lax.all_gather(student_head, "dp", axis=1, tiled=True),
    )
    student_normed = normalize(student_rows, student_gain)
    tokens = student_rows.shape[0]
    values = teacher_rows.astype(jnp.float32)
    squares = lax.psum(jnp.sum(values * values, axis=1), ("group", "mp"))
    scale = lax.rsqrt(squares / DT + epsilon)
    teacher_normed = (values * scale[:, None] * teacher_gain.astype(jnp.float32)).astype(
        jnp.bfloat16
    )
    teacher_logits = against(
        lax.all_gather(teacher_normed, ("group", "mp"), axis=1, tiled=True), head_teacher
    )
    student_logits = against(student_normed, head_student)
    teacher_top, student_top = lax.pmax(
        (jnp.max(teacher_logits, axis=1), jnp.max(student_logits, axis=1)), ("group", "mp")
    )
    teacher_sum, student_sum = lax.psum(
        (
            jnp.sum(jnp.exp(teacher_logits - teacher_top[:, None]), axis=1),
            jnp.sum(jnp.exp(student_logits - student_top[:, None]), axis=1),
        ),
        ("group", "mp"),
    )
    teacher_lse = teacher_top + jnp.log(teacher_sum)
    student_lse = student_top + jnp.log(student_sum)
    position = jnp.arange(tokens, dtype=jnp.int32) % LMAX
    live = (position < jnp.repeat(lengths, LMAX, total_repeat_length=tokens)).astype(jnp.float32)
    teacher_prob = jnp.exp(teacher_logits - teacher_lse[:, None])
    student_prob = jnp.exp(student_logits - student_lse[:, None])
    logit_grad = (live[:, None] * (student_prob - teacher_prob)).astype(jnp.bfloat16)
    head_grad = (
        lax.psum_scatter(
            lax.dot_general(
                student_normed,
                logit_grad,
                (((0,), (0,)), ((), ())),
                preferred_element_type=jnp.float32,
            ).astype(jnp.bfloat16),
            "dp",
            scatter_dimension=0,
            tiled=True,
        )
        .astype(jnp.float32)
        .T
    )
    rows = lax.slice_in_dim(
        logit_grad,
        0,
        tokens // lax.axis_size(("group", "mp")) * lax.axis_size(("group", "mp")),
        axis=0,
    )
    row_grad = lax.psum_scatter(
        jnp.dot(rows, head_student, preferred_element_type=jnp.float32).astype(jnp.bfloat16),
        ("group", "mp"),
        scatter_dimension=0,
        tiled=True,
    ).astype(jnp.float32)
    devices = lax.axis_size(("dp", "group", "mp"))
    head_square, row_square = lax.psum(
        (jnp.sum(head_grad * head_grad), jnp.sum(row_grad * row_grad)), ("dp", "group", "mp")
    )
    head_update = head_grad * lax.rsqrt(head_square / (head_grad.size * devices) + epsilon)
    row_update = row_grad * lax.rsqrt(row_square / (row_grad.size * devices) + epsilon)
    return (head_update.astype(jnp.bfloat16), row_update.astype(jnp.bfloat16))


MESH = pl.DeviceIdType.MESH
COLS = 2
CHUNKS = 3


def dot_nt(a, b):
    return lax.dot_general(a, b, (((1,), (1,)), ((), ())), preferred_element_type=jnp.float32)


def step_kernel(
    n_dp,
    t_rows, t_gain, t_head, s_rows, s_gain, s_head, lengths,
    head_out, row_out,
    rows_all, gain_all, ht, hs, srow, sn, tn, t_exp, s_exp, lg_t, lg,
    stat, stat_in, hx_out, hx_in, hz_out, hz_in, h_acc,
    rc_out, rc_in, ry_out, ry_in, r_acc, sq, sq_in, sq2, sq2_in,
    send_sem, recv_sem, local_sem,
):
    n_z = n_dp // COLS
    d, g, m = lax.axis_index("dp"), lax.axis_index("group"), lax.axis_index("mp")
    z, x = d // COLS, d % COLS
    px, pg, pm = 1 - x, 1 - g, 1 - m
    me = 2 * g + m
    voc, tf = t_head.shape
    sf = s_head.shape[1]
    tok, ds = s_rows.shape
    blocks = 4
    own = tok // blocks
    peers = [dict(group=g, mp=pm), dict(group=pg, mp=m), dict(group=pg, mp=pm)]
    peers_gm = [2 * g + pm, 2 * pg + m, 2 * pg + pm]

    barrier = pltpu.get_barrier_semaphore()
    for peer in peers:
        pl.semaphore_signal(barrier, inc=1, device_id=peer, device_id_type=MESH)
    for k in range(1, n_dp):
        pl.semaphore_signal(
            barrier, inc=1, device_id={"dp": (d + k) % n_dp}, device_id_type=MESH
        )

    locals_ = [
        pltpu.make_async_copy(src, dst, local_sem.at[i])
        for i, (src, dst) in enumerate(
            [
                (s_rows, srow),
                (t_rows, rows_all.at[me]),
                (t_head, ht.at[d]),
                (s_head, hs.at[d]),
            ]
        )
    ]
    for copy in locals_:
        copy.start()
    gain_all[me] = jnp.broadcast_to(
        t_gain[...].astype(jnp.float32).reshape(1, -1), gain_all.shape[1:]
    )
    pl.semaphore_wait(barrier, 3 + n_dp - 1)

    sent, always = [], None

    def send(src, dst, to, when=always):
        i = len(sent)
        copy = pltpu.make_async_remote_copy(
            src_ref=src, dst_ref=dst, send_sem=send_sem.at[i], recv_sem=recv_sem.at[i],
            device_id=to, device_id_type=MESH,
        )
        if when is None:
            copy.start()
        else:
            pl.when(when)(copy.start)
        sent.append((copy, when))
        return i

    def arrive(i, dst):
        pltpu.make_async_remote_copy(
            src_ref=dst, dst_ref=dst, send_sem=send_sem.at[i], recv_sem=recv_sem.at[i],
            device_id={"dp": d}, device_id_type=MESH,
        ).wait_recv()

    def col(k):
        return ((z + k) % n_z) * COLS + x

    to_x = {"dp": z * COLS + px}
    to_y = {"mp": pm}
    to_core = {"group": pg}
    piece = voc // CHUNKS

    def part(ref, c):
        return ref.at[pl.ds(c * piece, piece), :]

    parts = [(s_head, hs, None)] + [(t_head, ht, c) for c in range(CHUNKS)]
    ways = (1, -1)

    def view(ref, c):
        return ref if c is None else part(ref, c)

    def inside(at):
        return (at >= 0) & (at < n_z)

    along, across = {}, {}
    for p, (src, dst, c) in enumerate(parts):
        for way in ways:
            along[way, 0, p] = send(
                view(src, c), view(dst.at[d], c), {"dp": (z + way) % n_z * COLS + x},
                inside(z + way),
            )
        across[p] = send(view(src, c), view(dst.at[d], c), to_x)
        if p == 0:
            rows_y = send(t_rows, rows_all.at[me], to_y)
    rows_core = send(t_rows, rows_all.at[me], to_core)
    gains = [send(gain_all.at[me], gain_all.at[me], peer) for peer in peers]

    def origin(way, hop):
        return z - way * (hop + 1)

    def block(way, hop, column):
        return (origin(way, hop) + n_z) % n_z * COLS + column

    def forward(hop, p):
        _, dst, c = parts[p]
        for way in ways:
            here = inside(origin(way, hop))
            slot = view(dst.at[block(way, hop, x)], c)

            @pl.when(here)
            def _():
                arrive(along[way, hop, p], slot)

            if hop < n_z - 2:
                along[way, hop + 1, p] = send(
                    slot, slot, {"dp": (z + way + n_z) % n_z * COLS + x}, here & inside(z + way)
                )
            if hop == 0:
                across[way, hop, p] = send(slot, slot, to_x, here & ~from_end(way))
            elif hop < n_z - 2 or p not in bent:
                across[way, hop, p] = send(slot, slot, to_x, here)

    bent = (2, 3)
    turned, bend = {}, {}

    def from_end(way):
        return ~inside(origin(way, 0) - way)

    def arrive_if(when, i, dst):
        @pl.when(when)
        def _():
            arrive(i, dst)

    def turn(p):
        _, dst, c = parts[p]
        slot = view(dst.at[z * COLS + px], c)
        arrive(across[p], slot)
        for way in ways:
            turned[way, p] = send(
                slot, slot, {"dp": (z + way + n_z) % n_z * COLS + x},
                inside(z + way) & ~inside(z - way),
            )

    def through(hop, way):
        return inside(origin(way, hop)) & inside(z + way)

    def bend_on(p):
        _, dst, c = parts[p]
        for way in ways:
            slot = view(dst.at[block(way, n_z - 3, px)], c)
            arrive_if(through(n_z - 3, way), across[way, n_z - 3, p], slot)
            bend[way, p] = send(
                slot, slot, {"dp": (z + way + n_z) % n_z * COLS + x}, through(n_z - 3, way)
            )

    def arrive_across(way, hop, p):
        _, dst, c = parts[p]
        slot = view(dst.at[block(way, hop, px)], c)
        here = inside(origin(way, hop))
        if hop == 0:
            arrive_if(here & from_end(way), turned[way, p], slot)
            arrive_if(here & ~from_end(way), across[way, hop, p], slot)
        elif p not in bent or hop < n_z - 3:
            arrive_if(here, across[way, hop, p], slot)
        elif hop == n_z - 3:
            arrive_if(here & ~inside(z + way), across[way, hop, p], slot)
        else:
            arrive_if(here, bend[way, p], slot)

    locals_[0].wait()
    tile = 32

    gain = s_gain[...].astype(jnp.float32).reshape(1, -1)

    def student_tile(i, _):
        at = pl.ds(pl.multiple_of(i * tile, tile), tile)
        values = srow[at, :].astype(jnp.float32)
        mean_square = jnp.mean(values * values, axis=-1, keepdims=True)
        sn[at, :] = (values * lax.rsqrt(mean_square + epsilon) * gain).astype(jnp.bfloat16)
        return 0

    lax.fori_loop(0, tok // tile, student_tile, 0)

    for hop in range(n_z - 1):
        if hop == n_z - 2:
            for p in bent:
                bend_on(p)
        for p in range(len(parts)):
            forward(hop, p)
            if hop == 0:
                turn(p)
        if hop == n_z - 3:
            arrive(rows_y, rows_all.at[peers_gm[0]])
            rows_far = send(rows_all.at[peers_gm[0]], rows_all.at[peers_gm[0]], to_core)

    locals_[3].wait()
    for hop in range(n_z - 1):
        for way in ways:
            arrive_across(way, hop, 0)

    def student_block(f, _):
        at = pl.ds(pl.multiple_of(f * sf, sf), sf)
        s_exp[...] += dot_nt(hs[f], sn[:, at])
        return 0

    s_exp[...] = jnp.zeros_like(s_exp)
    lax.fori_loop(0, n_dp, student_block, 0)

    def softmax_part(ref, row):
        values = ref[...]
        top = jnp.max(values, axis=0, keepdims=True)
        exps = jnp.exp(values - top)
        ref[...] = exps
        stat[row : row + 1, :] = top
        stat[row + 1 : row + 2, :] = jnp.sum(exps, axis=0, keepdims=True)

    stat[...] = jnp.zeros_like(stat)
    softmax_part(s_exp, 0)

    locals_[1].wait()
    for i in range(3):
        arrive(gains[i], gain_all.at[peers_gm[i]])
    arrive(rows_core, rows_all.at[peers_gm[1]])
    arrive(rows_far, rows_all.at[peers_gm[2]])
    width = t_rows.shape[1]

    def teacher_tile(i, _):
        at = pl.ds(pl.multiple_of(i * tile, tile), tile)
        total = jnp.zeros((tile, 1), jnp.float32)
        for j in range(blocks):
            values = rows_all[j, at, :].astype(jnp.float32)
            total += jnp.sum(values * values, axis=-1, keepdims=True)
        scale = lax.rsqrt(total / (blocks * width) + epsilon)
        for j in range(blocks):
            values = rows_all[j, at, :].astype(jnp.float32)
            tn[j, at, :] = (values * scale * gain_all[j, 0:1, :]).astype(jnp.bfloat16)
        return 0

    lax.fori_loop(0, tok // tile, teacher_tile, 0)

    per = width // tf

    def teacher_block(f):
        at = pl.ds(pl.multiple_of((f % per) * tf, tf), tf)
        t_exp[...] += dot_nt(ht[f], tn[f // per, :, at])

    locals_[2].wait()
    t_exp[...] = jnp.zeros_like(t_exp)

    def own_column(i, _):
        teacher_block(i * COLS + x)
        return 0

    lax.fori_loop(0, n_z, own_column, 0)
    teacher_block(z * COLS + px)
    for hop in range(n_z - 1):
        for way in ways:
            for p in range(1, len(parts)):
                arrive_across(way, hop, p)

            @pl.when(inside(origin(way, hop)))
            def _():
                teacher_block(block(way, hop, px))

    softmax_part(t_exp, 2)

    stats = [send(stat, stat_in.at[i], peers[i]) for i in range(3)]
    for i in range(3):
        arrive(stats[i], stat_in.at[i])

    position = lax.broadcasted_iota(jnp.int32, (1, tok), 1) % LMAX
    live = (position < lengths[0]).astype(jnp.float32)

    def factor(row):
        tops = [stat[row : row + 1, :]] + [stat_in[i, row : row + 1, :] for i in range(3)]
        sums = [stat[row + 1 : row + 2, :]] + [
            stat_in[i, row + 1 : row + 2, :] for i in range(3)
        ]
        top = functools.reduce(jnp.maximum, tops)
        total = sum(s * jnp.exp(t - top) for s, t in zip(sums, tops))
        return live * jnp.exp(tops[0] - top - jnp.log(total))

    grad = s_exp[...] * factor(0) - t_exp[...] * factor(2)
    lg_t[...] = grad.astype(jnp.bfloat16)
    lg[...] = grad.T.astype(jnp.bfloat16)

    def head_block(f):
        at = pl.ds(pl.multiple_of(f * sf, sf), sf)
        return jnp.dot(lg_t[...], sn[:, at], preferred_element_type=jnp.float32)

    def row_block(t, dst, taken=None):
        at = pl.ds(pl.multiple_of(t * own, own), own)

        def step(f, _):
            to = pl.ds(pl.multiple_of(f * sf, sf), sf)
            value = jnp.dot(lg[at, :], hs[f], preferred_element_type=jnp.float32)
            if taken is not None:
                value += taken[:, to].astype(jnp.float32)
            dst[:, to] = value.astype(dst.dtype)
            return 0

        lax.fori_loop(0, n_dp, step, 0)

    def to_mate(i, mp):
        row_block(2 * pg + mp, rc_out.at[i])
        return send(rc_out.at[i], rc_in.at[i], to_core)

    order = [*range(1, n_z), 0]
    hx, hz = {}, {}
    rc = [to_mate(0, pm)]
    for k in order:
        hx_out[k] = head_block(((z + k) % n_z) * COLS + px).astype(jnp.bfloat16)
        hx[k] = send(hx_out.at[k], hx_in.at[k], to_x)
    rc.append(to_mate(1, m))
    arrive(rc[0], rc_in.at[0])
    row_block(2 * g + pm, ry_out, rc_in.at[0])
    ry = send(ry_out, ry_in, to_y)
    for k in order[:-1]:
        value = head_block(col(k))
        arrive(hx[k], hx_in.at[k])
        hz_out[k - 1] = (value + hx_in[k].astype(jnp.float32)).astype(jnp.bfloat16)
        hz[k] = send(hz_out.at[k - 1], hz_in.at[k - 1], {"dp": col(k)})
    value = head_block(d)
    arrive(hx[0], hx_in.at[0])
    h_acc[...] = value + hx_in[0].astype(jnp.float32)
    arrive(rc[1], rc_in.at[1])
    row_block(2 * g + m, r_acc, rc_in.at[1])
    for k in range(1, n_z):
        arrive(hz[k], hz_in.at[k - 1])
    total = h_acc[...] + sum(hz_in[k].astype(jnp.float32) for k in range(n_z - 1))
    h_acc[...] = total

    def fold(values):
        lanes = jnp.sum(values * values, axis=0, keepdims=True)
        return sum(lanes[:, i : i + 128] for i in range(0, lanes.shape[1], 128))

    sq[...] = jnp.zeros_like(sq)
    sq[0:1, :] = fold(total)
    arrive(ry, ry_in)

    def row_sum(i, acc):
        at = pl.ds(pl.multiple_of(i * tile, tile), tile)
        values = r_acc[at, :] + ry_in[at, :].astype(jnp.float32)
        r_acc[at, :] = values
        return acc + fold(values)

    sq[1:2, :] = lax.fori_loop(0, own // tile, row_sum, jnp.zeros((1, 128), jnp.float32))

    first = [send(sq, sq_in.at[i], peers[i]) for i in range(3)]
    for i in range(3):
        arrive(first[i], sq_in.at[i])
    sq2[...] = sq[...] + sq_in[0] + sq_in[1] + sq_in[2]
    second = [send(sq2, sq2_in.at[k - 1], {"dp": (d + k) % n_dp}) for k in range(1, n_dp)]
    for k in range(1, n_dp):
        arrive(second[k - 1], sq2_in.at[k - 1])
    squares = jnp.sum(sq2[...] + jnp.sum(sq2_in[...], axis=0), axis=1, keepdims=True)
    devices = n_dp * blocks
    head_out[...] = (
        h_acc[...] * lax.rsqrt(squares[0:1, :] / (voc * sf * devices) + epsilon)
    ).astype(jnp.bfloat16)
    row_out[...] = (
        r_acc[...] * lax.rsqrt(squares[1:2, :] / (own * ds * devices) + epsilon)
    ).astype(jnp.bfloat16)
    for copy, when in sent:
        if when is None:
            copy.wait_send()
        else:
            pl.when(when)(copy.wait_send)


def fused(
    teacher_rows, teacher_gain, teacher_head, student_rows, student_gain, student_head, lengths
):
    n_dp = lax.axis_size("dp")
    tok, width = teacher_rows.shape
    voc, tf = teacher_head.shape
    ds, sf = student_rows.shape[1], student_head.shape[1]
    n_z, own = n_dp // COLS, tok // 4
    bf, f32 = jnp.bfloat16, jnp.float32
    hops = (1 + CHUNKS) * ((n_z - 1) * 4 + 3)
    copies = 3 + hops + 3 + 3 + 2 * n_z - 1 + 3 + 3 + n_dp - 1
    anywhere, vmem = pl.BlockSpec(memory_space=pl.ANY), pl.BlockSpec(memory_space=pltpu.VMEM)
    scalars = pl.BlockSpec(memory_space=pltpu.SMEM)
    return pl.pallas_call(
        functools.partial(step_kernel, n_dp),
        out_shape=(
            jax.ShapeDtypeStruct((voc, sf), bf),
            jax.ShapeDtypeStruct((own, ds), bf),
        ),
        in_specs=[anywhere, vmem, anywhere, anywhere, vmem, anywhere, scalars],
        out_specs=(vmem, vmem),
        scratch_shapes=[
            pltpu.VMEM((4, tok, width), bf),
            pltpu.VMEM((4, 8, width), f32),
            pltpu.VMEM((n_dp, voc, tf), bf),
            pltpu.VMEM((n_dp, voc, sf), bf),
            pltpu.VMEM((tok, ds), bf),
            pltpu.VMEM((tok, ds), bf),
            pltpu.VMEM((4, tok, width), bf),
            pltpu.VMEM((voc, tok), f32),
            pltpu.VMEM((voc, tok), f32),
            pltpu.VMEM((voc, tok), bf),
            pltpu.VMEM((tok, voc), bf),
            pltpu.VMEM((8, tok), f32),
            pltpu.VMEM((3, 8, tok), f32),
            pltpu.VMEM((n_z, voc, sf), bf),
            pltpu.VMEM((n_z, voc, sf), bf),
            pltpu.VMEM((n_z - 1, voc, sf), bf),
            pltpu.VMEM((n_z - 1, voc, sf), bf),
            pltpu.VMEM((voc, sf), f32),
            pltpu.VMEM((2, own, ds), bf),
            pltpu.VMEM((2, own, ds), bf),
            pltpu.VMEM((own, ds), bf),
            pltpu.VMEM((own, ds), bf),
            pltpu.VMEM((own, ds), f32),
            pltpu.VMEM((8, 128), f32),
            pltpu.VMEM((3, 8, 128), f32),
            pltpu.VMEM((8, 128), f32),
            pltpu.VMEM((n_dp - 1, 8, 128), f32),
            pltpu.SemaphoreType.DMA((copies,)),
            pltpu.SemaphoreType.DMA((copies,)),
            pltpu.SemaphoreType.DMA((4,)),
        ],
        compiler_params=pltpu.CompilerParams(
            collective_id=0, has_side_effects=True, vmem_limit_bytes=56 << 20
        ),
    )(
        teacher_rows,
        teacher_gain,
        teacher_head,
        student_rows,
        student_gain,
        student_head,
        lengths,
    )


def step(*args):
    t_rows, _, t_head, s_rows, _, s_head, lengths = args
    fits = (
        (lax.axis_size("group"), lax.axis_size("mp"), lax.axis_size("dp") % COLS) == (2, 2, 0)
        and 4 * COLS <= lax.axis_size("dp") <= 16
        and t_head.shape[1] % 128 == 0
        and s_head.shape[1] % 128 == 0
        and t_rows.shape[1] % t_head.shape[1] == 0
        and t_head.shape[0] % (16 * CHUNKS) == 0
        and s_rows.shape[0] % 128 == 0
        and lengths.shape[0] == 1
    )
    return fused(*args) if fits else body(*args)


def solution(mesh):
    placed = (
        P("dp", ("group", "mp")),
        P(("group", "mp")),
        P(("group", "mp"), "dp"),
        P("dp", None),
        P(),
        P(("group", "mp"), "dp"),
        P("dp"),
    )
    return jax.shard_map(
        step,
        mesh=mesh,
        in_specs=placed,
        out_specs=(P(("group", "mp"), "dp"), P(("dp", "group", "mp"), None)),
        check_vma=False,
    )
```

```python
import functools

import jax
import jax.numpy as jnp
from jax import lax
from jax.experimental import pallas as pl
from jax.experimental.pallas import tpu as pltpu
from jax.sharding import PartitionSpec as P

DT = 5120
LMAX = 640


epsilon = 1e-06


def normalize(rows, gain):
    values = rows.astype(jnp.float32)
    mean_square = jnp.mean(values * values, axis=-1, keepdims=True)
    return (values * lax.rsqrt(mean_square + epsilon) * gain.astype(jnp.float32)).astype(
        jnp.bfloat16
    )


def against(rows, weights):
    return lax.dot_general(
        rows, weights, (((1,), (1,)), ((), ())), preferred_element_type=jnp.float32
    )


def body(
    teacher_rows, teacher_gain, teacher_head, student_rows, student_gain, student_head, lengths
):
    head_teacher, head_student = (
        lax.all_gather(teacher_head, "dp", axis=1, tiled=True),
        lax.all_gather(student_head, "dp", axis=1, tiled=True),
    )
    student_normed = normalize(student_rows, student_gain)
    tokens = student_rows.shape[0]
    values = teacher_rows.astype(jnp.float32)
    squares = lax.psum(jnp.sum(values * values, axis=1), ("group", "mp"))
    scale = lax.rsqrt(squares / DT + epsilon)
    teacher_normed = (values * scale[:, None] * teacher_gain.astype(jnp.float32)).astype(
        jnp.bfloat16
    )
    teacher_logits = against(
        lax.all_gather(teacher_normed, ("group", "mp"), axis=1, tiled=True), head_teacher
    )
    student_logits = against(student_normed, head_student)
    teacher_top, student_top = lax.pmax(
        (jnp.max(teacher_logits, axis=1), jnp.max(student_logits, axis=1)), ("group", "mp")
    )
    teacher_sum, student_sum = lax.psum(
        (
            jnp.sum(jnp.exp(teacher_logits - teacher_top[:, None]), axis=1),
            jnp.sum(jnp.exp(student_logits - student_top[:, None]), axis=1),
        ),
        ("group", "mp"),
    )
    teacher_lse = teacher_top + jnp.log(teacher_sum)
    student_lse = student_top + jnp.log(student_sum)
    position = jnp.arange(tokens, dtype=jnp.int32) % LMAX
    live = (position < jnp.repeat(lengths, LMAX, total_repeat_length=tokens)).astype(jnp.float32)
    teacher_prob = jnp.exp(teacher_logits - teacher_lse[:, None])
    student_prob = jnp.exp(student_logits - student_lse[:, None])
    logit_grad = (live[:, None] * (student_prob - teacher_prob)).astype(jnp.bfloat16)
    head_grad = (
        lax.psum_scatter(
            lax.dot_general(
                student_normed,
                logit_grad,
                (((0,), (0,)), ((), ())),
                preferred_element_type=jnp.float32,
            ).astype(jnp.bfloat16),
            "dp",
            scatter_dimension=0,
            tiled=True,
        )
        .astype(jnp.float32)
        .T
    )
    rows = lax.slice_in_dim(
        logit_grad,
        0,
        tokens // lax.axis_size(("group", "mp")) * lax.axis_size(("group", "mp")),
        axis=0,
    )
    row_grad = lax.psum_scatter(
        jnp.dot(rows, head_student, preferred_element_type=jnp.float32).astype(jnp.bfloat16),
        ("group", "mp"),
        scatter_dimension=0,
        tiled=True,
    ).astype(jnp.float32)
    devices = lax.axis_size(("dp", "group", "mp"))
    head_square, row_square = lax.psum(
        (jnp.sum(head_grad * head_grad), jnp.sum(row_grad * row_grad)), ("dp", "group", "mp")
    )
    head_update = head_grad * lax.rsqrt(head_square / (head_grad.size * devices) + epsilon)
    row_update = row_grad * lax.rsqrt(row_square / (row_grad.size * devices) + epsilon)
    return (head_update.astype(jnp.bfloat16), row_update.astype(jnp.bfloat16))


MESH = pl.DeviceIdType.MESH
COLS = 2
CHUNKS = 3


def dot_nt(a, b):
    return lax.dot_general(a, b, (((1,), (1,)), ((), ())), preferred_element_type=jnp.float32)


def step_kernel(
    n_dp,
    t_rows, t_gain, t_head, s_rows, s_gain, s_head, lengths,
    head_out, row_out,
    rows_all, gain_all, ht, hs, srow, sn, tn, t_exp, s_exp, lg_t, lg,
    stat, stat_in, hx_out, hx_in, hz_out, hz_in, h_acc,
    rc_out, rc_in, ry_out, ry_in, r_acc, sq, sq_in, sq2, sq2_in,
    send_sem, recv_sem, local_sem,
):
    n_z = n_dp // COLS
    d, g, m = lax.axis_index("dp"), lax.axis_index("group"), lax.axis_index("mp")
    z, x = d // COLS, d % COLS
    px, pg, pm = 1 - x, 1 - g, 1 - m
    me = 2 * g + m
    voc, tf = t_head.shape
    sf = s_head.shape[1]
    tok, ds = s_rows.shape
    blocks = 4
    own = tok // blocks
    peers = [dict(group=g, mp=pm), dict(group=pg, mp=m), dict(group=pg, mp=pm)]
    peers_gm = [2 * g + pm, 2 * pg + m, 2 * pg + pm]

    barrier = pltpu.get_barrier_semaphore()
    for peer in peers:
        pl.semaphore_signal(barrier, inc=1, device_id=peer, device_id_type=MESH)
    for k in range(1, n_dp):
        pl.semaphore_signal(
            barrier, inc=1, device_id={"dp": (d + k) % n_dp}, device_id_type=MESH
        )

    locals_ = [
        pltpu.make_async_copy(src, dst, local_sem.at[i])
        for i, (src, dst) in enumerate(
            [
                (s_rows, srow),
                (t_rows, rows_all.at[me]),
                (t_head, ht.at[d]),
                (s_head, hs.at[d]),
            ]
        )
    ]
    for copy in locals_:
        copy.start()
    gain_all[me] = jnp.broadcast_to(
        t_gain[...].astype(jnp.float32).reshape(1, -1), gain_all.shape[1:]
    )
    pl.semaphore_wait(barrier, 3 + n_dp - 1)

    sent, always = [], None

    def send(src, dst, to, when=always):
        i = len(sent)
        copy = pltpu.make_async_remote_copy(
            src_ref=src, dst_ref=dst, send_sem=send_sem.at[i], recv_sem=recv_sem.at[i],
            device_id=to, device_id_type=MESH,
        )
        if when is None:
            copy.start()
        else:
            pl.when(when)(copy.start)
        sent.append((copy, when))
        return i

    def arrive(i, dst):
        pltpu.make_async_remote_copy(
            src_ref=dst, dst_ref=dst, send_sem=send_sem.at[i], recv_sem=recv_sem.at[i],
            device_id={"dp": d}, device_id_type=MESH,
        ).wait_recv()

    def col(k):
        return ((z + k) % n_z) * COLS + x

    to_x = {"dp": z * COLS + px}
    to_y = {"mp": pm}
    to_core = {"group": pg}
    piece = voc // CHUNKS

    def part(ref, c):
        return ref.at[pl.ds(c * piece, piece), :]

    parts = [(s_head, hs, None)] + [(t_head, ht, c) for c in range(CHUNKS)]
    ways = (1, -1)

    def view(ref, c):
        return ref if c is None else part(ref, c)

    def inside(at):
        return (at >= 0) & (at < n_z)

    along, across = {}, {}
    for p, (src, dst, c) in enumerate(parts):
        for way in ways:
            along[way, 0, p] = send(
                view(src, c), view(dst.at[d], c), {"dp": (z + way) % n_z * COLS + x},
                inside(z + way),
            )
        across[p] = send(view(src, c), view(dst.at[d], c), to_x)
        if p == 0:
            rows_y = send(t_rows, rows_all.at[me], to_y)
    rows_core = send(t_rows, rows_all.at[me], to_core)
    gains = [send(gain_all.at[me], gain_all.at[me], peer) for peer in peers]

    def origin(way, hop):
        return z - way * (hop + 1)

    def block(way, hop, column):
        return (origin(way, hop) + n_z) % n_z * COLS + column

    def forward(hop, p):
        _, dst, c = parts[p]
        for way in ways:
            here = inside(origin(way, hop))
            slot = view(dst.at[block(way, hop, x)], c)

            @pl.when(here)
            def _():
                arrive(along[way, hop, p], slot)

            if hop < n_z - 2:
                along[way, hop + 1, p] = send(
                    slot, slot, {"dp": (z + way + n_z) % n_z * COLS + x}, here & inside(z + way)
                )
            if hop == 0:
                across[way, hop, p] = send(slot, slot, to_x, here & ~from_end(way))
            elif hop < n_z - 2 or p not in bent:
                across[way, hop, p] = send(slot, slot, to_x, here)

    bent = (2, 3)
    turned, bend = {}, {}

    def from_end(way):
        return ~inside(origin(way, 0) - way)

    def arrive_if(when, i, dst):
        @pl.when(when)
        def _():
            arrive(i, dst)

    def turn(p):
        _, dst, c = parts[p]
        slot = view(dst.at[z * COLS + px], c)
        arrive(across[p], slot)
        for way in ways:
            turned[way, p] = send(
                slot, slot, {"dp": (z + way + n_z) % n_z * COLS + x},
                inside(z + way) & ~inside(z - way),
            )

    def through(hop, way):
        return inside(origin(way, hop)) & inside(z + way)

    def bend_on(p):
        _, dst, c = parts[p]
        for way in ways:
            slot = view(dst.at[block(way, n_z - 3, px)], c)
            arrive_if(through(n_z - 3, way), across[way, n_z - 3, p], slot)
            bend[way, p] = send(
                slot, slot, {"dp": (z + way + n_z) % n_z * COLS + x}, through(n_z - 3, way)
            )

    def arrive_across(way, hop, p):
        _, dst, c = parts[p]
        slot = view(dst.at[block(way, hop, px)], c)
        here = inside(origin(way, hop))
        if hop == 0:
            arrive_if(here & from_end(way), turned[way, p], slot)
            arrive_if(here & ~from_end(way), across[way, hop, p], slot)
        elif p not in bent or hop < n_z - 3:
            arrive_if(here, across[way, hop, p], slot)
        elif hop == n_z - 3:
            arrive_if(here & ~inside(z + way), across[way, hop, p], slot)
        else:
            arrive_if(here, bend[way, p], slot)

    locals_[0].wait()
    tile = 32

    gain = s_gain[...].astype(jnp.float32).reshape(1, -1)

    def student_tile(i, _):
        at = pl.ds(pl.multiple_of(i * tile, tile), tile)
        values = srow[at, :].astype(jnp.float32)
        mean_square = jnp.mean(values * values, axis=-1, keepdims=True)
        sn[at, :] = (values * lax.rsqrt(mean_square + epsilon) * gain).astype(jnp.bfloat16)
        return 0

    lax.fori_loop(0, tok // tile, student_tile, 0)

    def student_block(f):
        at = pl.ds(pl.multiple_of(f * sf, sf), sf)
        s_exp[...] += dot_nt(hs[f], sn[:, at])

    def student_blocks(which):
        def step(i, _):
            @pl.when(which(i))
            def _():
                student_block(i * COLS + x)
                student_block(i * COLS + px)

            return 0

        lax.fori_loop(0, n_z, step, 0)

    def softmax_part(ref, row):
        values = ref[...]
        top = jnp.max(values, axis=0, keepdims=True)
        exps = jnp.exp(values - top)
        ref[...] = exps
        stat[row : row + 1, :] = top
        stat[row + 1 : row + 2, :] = jnp.sum(exps, axis=0, keepdims=True)

    for hop in range(n_z - 2):
        for p in range(len(parts)):
            forward(hop, p)
            if hop == 0:
                turn(p)
    arrive(rows_y, rows_all.at[peers_gm[0]])
    rows_far = send(rows_all.at[peers_gm[0]], rows_all.at[peers_gm[0]], to_core)

    near = n_z - 2
    locals_[3].wait()
    for hop in range(near):
        for way in ways:
            arrive_across(way, hop, 0)
    s_exp[...] = jnp.zeros_like(s_exp)
    student_blocks(lambda i: (i - z <= near) & (z - i <= near))
    locals_[1].wait()
    for i in range(3):
        arrive(gains[i], gain_all.at[peers_gm[i]])
    arrive(rows_core, rows_all.at[peers_gm[1]])
    arrive(rows_far, rows_all.at[peers_gm[2]])
    width = t_rows.shape[1]

    def teacher_tile(i, _):
        at = pl.ds(pl.multiple_of(i * tile, tile), tile)
        total = jnp.zeros((tile, 1), jnp.float32)
        for j in range(blocks):
            values = rows_all[j, at, :].astype(jnp.float32)
            total += jnp.sum(values * values, axis=-1, keepdims=True)
        scale = lax.rsqrt(total / (blocks * width) + epsilon)
        for j in range(blocks):
            values = rows_all[j, at, :].astype(jnp.float32)
            tn[j, at, :] = (values * scale * gain_all[j, 0:1, :]).astype(jnp.bfloat16)
        return 0

    lax.fori_loop(0, tok // tile, teacher_tile, 0)

    for p in bent:
        bend_on(p)
    for p in range(len(parts)):
        forward(near, p)
    for way in ways:
        arrive_across(way, near, 0)
    student_blocks(lambda i: (i - z > near) | (z - i > near))
    stat[...] = jnp.zeros_like(stat)
    softmax_part(s_exp, 0)

    per = width // tf

    def teacher_block(f):
        at = pl.ds(pl.multiple_of((f % per) * tf, tf), tf)
        t_exp[...] += dot_nt(ht[f], tn[f // per, :, at])

    locals_[2].wait()
    t_exp[...] = jnp.zeros_like(t_exp)

    def own_column(i, _):
        teacher_block(i * COLS + x)
        return 0

    lax.fori_loop(0, n_z, own_column, 0)
    teacher_block(z * COLS + px)
    for hop in range(n_z - 1):
        for way in ways:
            for p in range(1, len(parts)):
                arrive_across(way, hop, p)

            @pl.when(inside(origin(way, hop)))
            def _():
                teacher_block(block(way, hop, px))

    softmax_part(t_exp, 2)

    stats = [send(stat, stat_in.at[i], peers[i]) for i in range(3)]
    for i in range(3):
        arrive(stats[i], stat_in.at[i])

    position = lax.broadcasted_iota(jnp.int32, (1, tok), 1) % LMAX
    live = (position < lengths[0]).astype(jnp.float32)

    def factor(row):
        tops = [stat[row : row + 1, :]] + [stat_in[i, row : row + 1, :] for i in range(3)]
        sums = [stat[row + 1 : row + 2, :]] + [
            stat_in[i, row + 1 : row + 2, :] for i in range(3)
        ]
        top = functools.reduce(jnp.maximum, tops)
        total = sum(s * jnp.exp(t - top) for s, t in zip(sums, tops))
        return live * jnp.exp(tops[0] - top - jnp.log(total))

    grad = s_exp[...] * factor(0) - t_exp[...] * factor(2)
    lg_t[...] = grad.astype(jnp.bfloat16)
    lg[...] = grad.T.astype(jnp.bfloat16)

    def head_block(f):
        at = pl.ds(pl.multiple_of(f * sf, sf), sf)
        return jnp.dot(lg_t[...], sn[:, at], preferred_element_type=jnp.float32)

    def row_block(t, dst, taken=None):
        at = pl.ds(pl.multiple_of(t * own, own), own)

        def step(f, _):
            to = pl.ds(pl.multiple_of(f * sf, sf), sf)
            value = jnp.dot(lg[at, :], hs[f], preferred_element_type=jnp.float32)
            if taken is not None:
                value += taken[:, to].astype(jnp.float32)
            dst[:, to] = value.astype(dst.dtype)
            return 0

        lax.fori_loop(0, n_dp, step, 0)

    def to_mate(i, mp):
        row_block(2 * pg + mp, rc_out.at[i])
        return send(rc_out.at[i], rc_in.at[i], to_core)

    order = [*range(1, n_z), 0]
    hx, hz = {}, {}
    rc = []
    for k in order:
        hx_out[k] = head_block(((z + k) % n_z) * COLS + px).astype(jnp.bfloat16)
        hx[k] = send(hx_out.at[k], hx_in.at[k], to_x)
        if not rc:
            rc.append(to_mate(0, pm))
    rc.append(to_mate(1, m))
    arrive(rc[0], rc_in.at[0])
    row_block(2 * g + pm, ry_out, rc_in.at[0])
    ry = send(ry_out, ry_in, to_y)
    for k in order[:-1]:
        value = head_block(col(k))
        arrive(hx[k], hx_in.at[k])
        hz_out[k - 1] = (value + hx_in[k].astype(jnp.float32)).astype(jnp.bfloat16)
        hz[k] = send(hz_out.at[k - 1], hz_in.at[k - 1], {"dp": col(k)})
    value = head_block(d)
    arrive(hx[0], hx_in.at[0])
    h_acc[...] = value + hx_in[0].astype(jnp.float32)
    arrive(rc[1], rc_in.at[1])
    row_block(2 * g + m, r_acc, rc_in.at[1])
    for k in range(1, n_z):
        arrive(hz[k], hz_in.at[k - 1])
    total = h_acc[...] + sum(hz_in[k].astype(jnp.float32) for k in range(n_z - 1))
    h_acc[...] = total

    def fold(values):
        lanes = jnp.sum(values * values, axis=0, keepdims=True)
        return sum(lanes[:, i : i + 128] for i in range(0, lanes.shape[1], 128))

    sq[...] = jnp.zeros_like(sq)
    sq[0:1, :] = fold(total)
    arrive(ry, ry_in)

    def row_sum(i, acc):
        at = pl.ds(pl.multiple_of(i * tile, tile), tile)
        values = r_acc[at, :] + ry_in[at, :].astype(jnp.float32)
        r_acc[at, :] = values
        return acc + fold(values)

    sq[1:2, :] = lax.fori_loop(0, own // tile, row_sum, jnp.zeros((1, 128), jnp.float32))

    first = [send(sq, sq_in.at[i], peers[i]) for i in range(3)]
    for i in range(3):
        arrive(first[i], sq_in.at[i])
    sq2[...] = sq[...] + sq_in[0] + sq_in[1] + sq_in[2]
    second = [send(sq2, sq2_in.at[k - 1], {"dp": (d + k) % n_dp}) for k in range(1, n_dp)]
    for k in range(1, n_dp):
        arrive(second[k - 1], sq2_in.at[k - 1])
    squares = jnp.sum(sq2[...] + jnp.sum(sq2_in[...], axis=0), axis=1, keepdims=True)
    devices = n_dp * blocks
    head_out[...] = (
        h_acc[...] * lax.rsqrt(squares[0:1, :] / (voc * sf * devices) + epsilon)
    ).astype(jnp.bfloat16)
    row_out[...] = (
        r_acc[...] * lax.rsqrt(squares[1:2, :] / (own * ds * devices) + epsilon)
    ).astype(jnp.bfloat16)
    for copy, when in sent:
        if when is None:
            copy.wait_send()
        else:
            pl.when(when)(copy.wait_send)


def fused(
    teacher_rows, teacher_gain, teacher_head, student_rows, student_gain, student_head, lengths
):
    n_dp = lax.axis_size("dp")
    tok, width = teacher_rows.shape
    voc, tf = teacher_head.shape
    ds, sf = student_rows.shape[1], student_head.shape[1]
    n_z, own = n_dp // COLS, tok // 4
    bf, f32 = jnp.bfloat16, jnp.float32
    hops = (1 + CHUNKS) * ((n_z - 1) * 4 + 3)
    copies = 3 + hops + 3 + 3 + 2 * n_z - 1 + 3 + 3 + n_dp - 1
    anywhere, vmem = pl.BlockSpec(memory_space=pl.ANY), pl.BlockSpec(memory_space=pltpu.VMEM)
    scalars = pl.BlockSpec(memory_space=pltpu.SMEM)
    return pl.pallas_call(
        functools.partial(step_kernel, n_dp),
        out_shape=(
            jax.ShapeDtypeStruct((voc, sf), bf),
            jax.ShapeDtypeStruct((own, ds), bf),
        ),
        in_specs=[anywhere, vmem, anywhere, anywhere, vmem, anywhere, scalars],
        out_specs=(vmem, vmem),
        scratch_shapes=[
            pltpu.VMEM((4, tok, width), bf),
            pltpu.VMEM((4, 8, width), f32),
            pltpu.VMEM((n_dp, voc, tf), bf),
            pltpu.VMEM((n_dp, voc, sf), bf),
            pltpu.VMEM((tok, ds), bf),
            pltpu.VMEM((tok, ds), bf),
            pltpu.VMEM((4, tok, width), bf),
            pltpu.VMEM((voc, tok), f32),
            pltpu.VMEM((voc, tok), f32),
            pltpu.VMEM((voc, tok), bf),
            pltpu.VMEM((tok, voc), bf),
            pltpu.VMEM((8, tok), f32),
            pltpu.VMEM((3, 8, tok), f32),
            pltpu.VMEM((n_z, voc, sf), bf),
            pltpu.VMEM((n_z, voc, sf), bf),
            pltpu.VMEM((n_z - 1, voc, sf), bf),
            pltpu.VMEM((n_z - 1, voc, sf), bf),
            pltpu.VMEM((voc, sf), f32),
            pltpu.VMEM((2, own, ds), bf),
            pltpu.VMEM((2, own, ds), bf),
            pltpu.VMEM((own, ds), bf),
            pltpu.VMEM((own, ds), bf),
            pltpu.VMEM((own, ds), f32),
            pltpu.VMEM((8, 128), f32),
            pltpu.VMEM((3, 8, 128), f32),
            pltpu.VMEM((8, 128), f32),
            pltpu.VMEM((n_dp - 1, 8, 128), f32),
            pltpu.SemaphoreType.DMA((copies,)),
            pltpu.SemaphoreType.DMA((copies,)),
            pltpu.SemaphoreType.DMA((4,)),
        ],
        compiler_params=pltpu.CompilerParams(
            collective_id=0, has_side_effects=True, vmem_limit_bytes=56 << 20
        ),
    )(
        teacher_rows,
        teacher_gain,
        teacher_head,
        student_rows,
        student_gain,
        student_head,
        lengths,
    )


def step(*args):
    t_rows, _, t_head, s_rows, _, s_head, lengths = args
    fits = (
        (lax.axis_size("group"), lax.axis_size("mp"), lax.axis_size("dp") % COLS) == (2, 2, 0)
        and 4 * COLS <= lax.axis_size("dp") <= 16
        and t_head.shape[1] % 128 == 0
        and s_head.shape[1] % 128 == 0
        and t_rows.shape[1] % t_head.shape[1] == 0
        and t_head.shape[0] % (16 * CHUNKS) == 0
        and s_rows.shape[0] % 128 == 0
        and lengths.shape[0] == 1
    )
    return fused(*args) if fits else body(*args)


def solution(mesh):
    placed = (
        P("dp", ("group", "mp")),
        P(("group", "mp")),
        P(("group", "mp"), "dp"),
        P("dp", None),
        P(),
        P(("group", "mp"), "dp"),
        P("dp"),
    )
    return jax.shard_map(
        step,
        mesh=mesh,
        in_specs=placed,
        out_specs=(P(("group", "mp"), "dp"), P(("dp", "group", "mp"), None)),
        check_vma=False,
    )
```

```python
import functools

import jax
import jax.numpy as jnp
from jax import lax
from jax.experimental import pallas as pl
from jax.experimental.pallas import tpu as pltpu
from jax.sharding import PartitionSpec as P

DT = 5120
LMAX = 640


epsilon = 1e-06


def normalize(rows, gain):
    values = rows.astype(jnp.float32)
    mean_square = jnp.mean(values * values, axis=-1, keepdims=True)
    return (values * lax.rsqrt(mean_square + epsilon) * gain.astype(jnp.float32)).astype(
        jnp.bfloat16
    )


def against(rows, weights):
    return lax.dot_general(
        rows, weights, (((1,), (1,)), ((), ())), preferred_element_type=jnp.float32
    )


def body(
    teacher_rows, teacher_gain, teacher_head, student_rows, student_gain, student_head, lengths
):
    head_teacher, head_student = (
        lax.all_gather(teacher_head, "dp", axis=1, tiled=True),
        lax.all_gather(student_head, "dp", axis=1, tiled=True),
    )
    student_normed = normalize(student_rows, student_gain)
    tokens = student_rows.shape[0]
    values = teacher_rows.astype(jnp.float32)
    squares = lax.psum(jnp.sum(values * values, axis=1), ("group", "mp"))
    scale = lax.rsqrt(squares / DT + epsilon)
    teacher_normed = (values * scale[:, None] * teacher_gain.astype(jnp.float32)).astype(
        jnp.bfloat16
    )
    teacher_logits = against(
        lax.all_gather(teacher_normed, ("group", "mp"), axis=1, tiled=True), head_teacher
    )
    student_logits = against(student_normed, head_student)
    teacher_top, student_top = lax.pmax(
        (jnp.max(teacher_logits, axis=1), jnp.max(student_logits, axis=1)), ("group", "mp")
    )
    teacher_sum, student_sum = lax.psum(
        (
            jnp.sum(jnp.exp(teacher_logits - teacher_top[:, None]), axis=1),
            jnp.sum(jnp.exp(student_logits - student_top[:, None]), axis=1),
        ),
        ("group", "mp"),
    )
    teacher_lse = teacher_top + jnp.log(teacher_sum)
    student_lse = student_top + jnp.log(student_sum)
    position = jnp.arange(tokens, dtype=jnp.int32) % LMAX
    live = (position < jnp.repeat(lengths, LMAX, total_repeat_length=tokens)).astype(jnp.float32)
    teacher_prob = jnp.exp(teacher_logits - teacher_lse[:, None])
    student_prob = jnp.exp(student_logits - student_lse[:, None])
    logit_grad = (live[:, None] * (student_prob - teacher_prob)).astype(jnp.bfloat16)
    head_grad = (
        lax.psum_scatter(
            lax.dot_general(
                student_normed,
                logit_grad,
                (((0,), (0,)), ((), ())),
                preferred_element_type=jnp.float32,
            ).astype(jnp.bfloat16),
            "dp",
            scatter_dimension=0,
            tiled=True,
        )
        .astype(jnp.float32)
        .T
    )
    rows = lax.slice_in_dim(
        logit_grad,
        0,
        tokens // lax.axis_size(("group", "mp")) * lax.axis_size(("group", "mp")),
        axis=0,
    )
    row_grad = lax.psum_scatter(
        jnp.dot(rows, head_student, preferred_element_type=jnp.float32).astype(jnp.bfloat16),
        ("group", "mp"),
        scatter_dimension=0,
        tiled=True,
    ).astype(jnp.float32)
    devices = lax.axis_size(("dp", "group", "mp"))
    head_square, row_square = lax.psum(
        (jnp.sum(head_grad * head_grad), jnp.sum(row_grad * row_grad)), ("dp", "group", "mp")
    )
    head_update = head_grad * lax.rsqrt(head_square / (head_grad.size * devices) + epsilon)
    row_update = row_grad * lax.rsqrt(row_square / (row_grad.size * devices) + epsilon)
    return (head_update.astype(jnp.bfloat16), row_update.astype(jnp.bfloat16))


MESH = pl.DeviceIdType.MESH
COLS = 2
CHUNKS = 3


def dot_nt(a, b):
    return lax.dot_general(a, b, (((1,), (1,)), ((), ())), preferred_element_type=jnp.float32)


def step_kernel(
    n_dp,
    t_rows, t_gain, t_head, s_rows, s_gain, s_head, lengths,
    h_acc, r_acc, squares,
    rows_all, gain_all, ht, hs, srow, sn, tn, t_exp, s_exp, lg_t, lg,
    stat, stat_in, hx_out, hx_in, hz_out, hz_in,
    rc_out, rc_in, ry_out, ry_in, sq, sq_in, sq2, sq2_in,
    send_sem, recv_sem, local_sem,
):
    n_z = n_dp // COLS
    d, g, m = lax.axis_index("dp"), lax.axis_index("group"), lax.axis_index("mp")
    z, x = d // COLS, d % COLS
    px, pg, pm = 1 - x, 1 - g, 1 - m
    me = 2 * g + m
    voc, tf = t_head.shape
    sf = s_head.shape[1]
    tok, ds = s_rows.shape
    blocks = 4
    own = tok // blocks
    peers = [dict(group=g, mp=pm), dict(group=pg, mp=m), dict(group=pg, mp=pm)]
    peers_gm = [2 * g + pm, 2 * pg + m, 2 * pg + pm]

    barrier = pltpu.get_barrier_semaphore()
    for peer in peers:
        pl.semaphore_signal(barrier, inc=1, device_id=peer, device_id_type=MESH)
    for k in range(1, n_dp):
        pl.semaphore_signal(
            barrier, inc=1, device_id={"dp": (d + k) % n_dp}, device_id_type=MESH
        )

    locals_ = [
        pltpu.make_async_copy(src, dst, local_sem.at[i])
        for i, (src, dst) in enumerate(
            [
                (s_rows, srow),
                (t_rows, rows_all.at[me]),
                (t_head, ht.at[d]),
                (s_head, hs.at[d]),
            ]
        )
    ]
    for copy in locals_:
        copy.start()
    gain_all[me] = jnp.broadcast_to(
        t_gain[...].astype(jnp.float32).reshape(1, -1), gain_all.shape[1:]
    )
    pl.semaphore_wait(barrier, 3 + n_dp - 1)

    sent, always = [], None

    def send(src, dst, to, when=always):
        i = len(sent)
        copy = pltpu.make_async_remote_copy(
            src_ref=src, dst_ref=dst, send_sem=send_sem.at[i], recv_sem=recv_sem.at[i],
            device_id=to, device_id_type=MESH,
        )
        if when is None:
            copy.start()
        else:
            pl.when(when)(copy.start)
        sent.append((copy, when))
        return i

    def arrive(i, dst):
        pltpu.make_async_remote_copy(
            src_ref=dst, dst_ref=dst, send_sem=send_sem.at[i], recv_sem=recv_sem.at[i],
            device_id={"dp": d}, device_id_type=MESH,
        ).wait_recv()

    def col(k):
        return ((z + k) % n_z) * COLS + x

    to_x = {"dp": z * COLS + px}
    to_y = {"mp": pm}
    to_core = {"group": pg}
    piece = voc // CHUNKS

    def part(ref, c):
        return ref.at[pl.ds(c * piece, piece), :]

    parts = [(s_head, hs, None)] + [(t_head, ht, c) for c in range(CHUNKS)]
    ways = (1, -1)

    def view(ref, c):
        return ref if c is None else part(ref, c)

    def inside(at):
        return (at >= 0) & (at < n_z)

    along, across = {}, {}
    for p, (src, dst, c) in enumerate(parts):
        for way in ways:
            along[way, 0, p] = send(
                view(src, c), view(dst.at[d], c), {"dp": (z + way) % n_z * COLS + x},
                inside(z + way),
            )
        across[p] = send(view(src, c), view(dst.at[d], c), to_x)
        if p == 0:
            rows_y = send(t_rows, rows_all.at[me], to_y)
    rows_core = send(t_rows, rows_all.at[me], to_core)
    gains = [send(gain_all.at[me], gain_all.at[me], peer) for peer in peers]

    def origin(way, hop):
        return z - way * (hop + 1)

    def block(way, hop, column):
        return (origin(way, hop) + n_z) % n_z * COLS + column

    def forward(hop, p):
        _, dst, c = parts[p]
        for way in ways:
            here = inside(origin(way, hop))
            slot = view(dst.at[block(way, hop, x)], c)

            @pl.when(here)
            def _():
                arrive(along[way, hop, p], slot)

            if hop < n_z - 2:
                along[way, hop + 1, p] = send(
                    slot, slot, {"dp": (z + way + n_z) % n_z * COLS + x}, here & inside(z + way)
                )
            if hop == 0:
                across[way, hop, p] = send(slot, slot, to_x, here & ~from_end(way))
            elif hop < n_z - 2 or p not in bent:
                across[way, hop, p] = send(slot, slot, to_x, here)

    bent = (2, 3)
    turned, bend = {}, {}

    def from_end(way):
        return ~inside(origin(way, 0) - way)

    def arrive_if(when, i, dst):
        @pl.when(when)
        def _():
            arrive(i, dst)

    def turn(p):
        _, dst, c = parts[p]
        slot = view(dst.at[z * COLS + px], c)
        arrive(across[p], slot)
        for way in ways:
            turned[way, p] = send(
                slot, slot, {"dp": (z + way + n_z) % n_z * COLS + x},
                inside(z + way) & ~inside(z - way),
            )

    def through(hop, way):
        return inside(origin(way, hop)) & inside(z + way)

    def bend_on(p):
        _, dst, c = parts[p]
        for way in ways:
            slot = view(dst.at[block(way, n_z - 3, px)], c)
            arrive_if(through(n_z - 3, way), across[way, n_z - 3, p], slot)
            bend[way, p] = send(
                slot, slot, {"dp": (z + way + n_z) % n_z * COLS + x}, through(n_z - 3, way)
            )

    def arrive_across(way, hop, p):
        _, dst, c = parts[p]
        slot = view(dst.at[block(way, hop, px)], c)
        here = inside(origin(way, hop))
        if hop == 0:
            arrive_if(here & from_end(way), turned[way, p], slot)
            arrive_if(here & ~from_end(way), across[way, hop, p], slot)
        elif p not in bent or hop < n_z - 3:
            arrive_if(here, across[way, hop, p], slot)
        elif hop == n_z - 3:
            arrive_if(here & ~inside(z + way), across[way, hop, p], slot)
        else:
            arrive_if(here, bend[way, p], slot)

    locals_[0].wait()
    tile = 32

    gain = s_gain[...].astype(jnp.float32).reshape(1, -1)

    def student_tile(i, _):
        at = pl.ds(pl.multiple_of(i * tile, tile), tile)
        values = srow[at, :].astype(jnp.float32)
        mean_square = jnp.mean(values * values, axis=-1, keepdims=True)
        sn[at, :] = (values * lax.rsqrt(mean_square + epsilon) * gain).astype(jnp.bfloat16)
        return 0

    lax.fori_loop(0, tok // tile, student_tile, 0)

    def student_block(f):
        at = pl.ds(pl.multiple_of(f * sf, sf), sf)
        s_exp[...] += dot_nt(hs[f], sn[:, at])

    def student_blocks(which):
        def step(i, _):
            @pl.when(which(i))
            def _():
                student_block(i * COLS + x)
                student_block(i * COLS + px)

            return 0

        lax.fori_loop(0, n_z, step, 0)

    def softmax_part(ref, row):
        values = ref[...]
        top = jnp.max(values, axis=0, keepdims=True)
        exps = jnp.exp(values - top)
        ref[...] = exps
        stat[row : row + 1, :] = top
        stat[row + 1 : row + 2, :] = jnp.sum(exps, axis=0, keepdims=True)

    for hop in range(n_z - 2):
        for p in range(len(parts)):
            forward(hop, p)
            if hop == 0:
                turn(p)
    arrive(rows_y, rows_all.at[peers_gm[0]])
    rows_far = send(rows_all.at[peers_gm[0]], rows_all.at[peers_gm[0]], to_core)

    near = n_z - 2
    locals_[3].wait()
    for hop in range(near):
        for way in ways:
            arrive_across(way, hop, 0)
    s_exp[...] = jnp.zeros_like(s_exp)
    student_blocks(lambda i: (i - z <= near) & (z - i <= near))
    locals_[1].wait()
    for i in range(3):
        arrive(gains[i], gain_all.at[peers_gm[i]])
    arrive(rows_core, rows_all.at[peers_gm[1]])
    arrive(rows_far, rows_all.at[peers_gm[2]])
    width = t_rows.shape[1]

    def teacher_tile(i, _):
        at = pl.ds(pl.multiple_of(i * tile, tile), tile)
        total = jnp.zeros((tile, 1), jnp.float32)
        for j in range(blocks):
            values = rows_all[j, at, :].astype(jnp.float32)
            total += jnp.sum(values * values, axis=-1, keepdims=True)
        scale = lax.rsqrt(total / (blocks * width) + epsilon)
        for j in range(blocks):
            values = rows_all[j, at, :].astype(jnp.float32)
            tn[j, at, :] = (values * scale * gain_all[j, 0:1, :]).astype(jnp.bfloat16)
        return 0

    lax.fori_loop(0, tok // tile, teacher_tile, 0)

    for p in bent:
        bend_on(p)
    for p in range(len(parts)):
        forward(near, p)
    for way in ways:
        arrive_across(way, near, 0)
    student_blocks(lambda i: (i - z > near) | (z - i > near))
    stat[...] = jnp.zeros_like(stat)
    softmax_part(s_exp, 0)

    per = width // tf

    def teacher_block(f):
        at = pl.ds(pl.multiple_of((f % per) * tf, tf), tf)
        t_exp[...] += dot_nt(ht[f], tn[f // per, :, at])

    locals_[2].wait()
    t_exp[...] = jnp.zeros_like(t_exp)

    def own_column(i, _):
        teacher_block(i * COLS + x)
        return 0

    lax.fori_loop(0, n_z, own_column, 0)
    teacher_block(z * COLS + px)
    for hop in range(n_z - 1):
        for way in ways:
            for p in range(1, len(parts)):
                arrive_across(way, hop, p)

            @pl.when(inside(origin(way, hop)))
            def _():
                teacher_block(block(way, hop, px))

    softmax_part(t_exp, 2)

    stats = [send(stat, stat_in.at[i], peers[i]) for i in range(3)]
    for i in range(3):
        arrive(stats[i], stat_in.at[i])

    position = lax.broadcasted_iota(jnp.int32, (1, tok), 1) % LMAX
    live = (position < lengths[0]).astype(jnp.float32)

    def factor(row):
        tops = [stat[row : row + 1, :]] + [stat_in[i, row : row + 1, :] for i in range(3)]
        sums = [stat[row + 1 : row + 2, :]] + [
            stat_in[i, row + 1 : row + 2, :] for i in range(3)
        ]
        top = functools.reduce(jnp.maximum, tops)
        total = sum(s * jnp.exp(t - top) for s, t in zip(sums, tops))
        return live * jnp.exp(tops[0] - top - jnp.log(total))

    grad = s_exp[...] * factor(0) - t_exp[...] * factor(2)
    lg_t[...] = grad.astype(jnp.bfloat16)

    def head_block(f):
        at = pl.ds(pl.multiple_of(f * sf, sf), sf)
        return jnp.dot(lg_t[...], sn[:, at], preferred_element_type=jnp.float32)

    def row_block(t, dst, taken=None):
        at = pl.ds(pl.multiple_of(t * own, own), own)

        def step(f, _):
            to = pl.ds(pl.multiple_of(f * sf, sf), sf)
            value = jnp.dot(lg[at, :], hs[f], preferred_element_type=jnp.float32)
            if taken is not None:
                value += taken[:, to].astype(jnp.float32)
            dst[:, to] = value.astype(dst.dtype)
            return 0

        lax.fori_loop(0, n_dp, step, 0)

    def to_mate():
        at = pl.ds(pl.multiple_of(2 * pg * own, own), 2 * own)

        def step(f, _):
            to = pl.ds(pl.multiple_of(f * sf, sf), sf)
            value = jnp.dot(lg[at, :], hs[f], preferred_element_type=jnp.float32)
            value = value.astype(jnp.bfloat16)
            rc_out[0, :, to] = value[:own]
            rc_out[1, :, to] = value[own:]
            return 0

        lax.fori_loop(0, n_dp, step, 0)
        return [send(rc_out.at[mp], rc_in.at[mp], to_core) for mp in (pm, m)]

    order = [*range(1, n_z), 0]
    hx, hz = {}, {}
    for k in order:
        hx_out[k] = head_block(((z + k) % n_z) * COLS + px).astype(jnp.bfloat16)
        hx[k] = send(hx_out.at[k], hx_in.at[k], to_x)
        if k == order[0]:
            lg[...] = lg_t[...].T
            rc = to_mate()
    arrive(rc[0], rc_in.at[pm])
    row_block(2 * g + pm, ry_out, rc_in.at[pm])
    ry = send(ry_out, ry_in, to_y)
    for k in order[:-1]:
        value = head_block(col(k))
        arrive(hx[k], hx_in.at[k])
        hz_out[k - 1] = (value + hx_in[k].astype(jnp.float32)).astype(jnp.bfloat16)
        hz[k] = send(hz_out.at[k - 1], hz_in.at[k - 1], {"dp": col(k)})
    value = head_block(d)
    arrive(hx[0], hx_in.at[0])
    h_acc[...] = value + hx_in[0].astype(jnp.float32)
    arrive(rc[1], rc_in.at[m])
    row_block(2 * g + m, r_acc, rc_in.at[m])
    for k in range(1, n_z):
        arrive(hz[k], hz_in.at[k - 1])
    total = h_acc[...] + sum(hz_in[k].astype(jnp.float32) for k in range(n_z - 1))
    h_acc[...] = total

    def fold(values):
        lanes = jnp.sum(values * values, axis=0, keepdims=True)
        return sum(lanes[:, i : i + 128] for i in range(0, lanes.shape[1], 128))

    sq[...] = jnp.zeros_like(sq)
    sq[0:1, :] = fold(total)
    arrive(ry, ry_in)

    def row_sum(i, acc):
        at = pl.ds(pl.multiple_of(i * tile, tile), tile)
        values = r_acc[at, :] + ry_in[at, :].astype(jnp.float32)
        r_acc[at, :] = values
        return acc + fold(values)

    sq[1:2, :] = lax.fori_loop(0, own // tile, row_sum, jnp.zeros((1, 128), jnp.float32))

    first = [send(sq, sq_in.at[i], peers[i]) for i in range(3)]
    for i in range(3):
        arrive(first[i], sq_in.at[i])
    sq2[...] = sq[...] + sq_in[0] + sq_in[1] + sq_in[2]
    second = [send(sq2, sq2_in.at[k - 1], {"dp": (d + k) % n_dp}) for k in range(1, n_dp)]
    for k in range(1, n_dp):
        arrive(second[k - 1], sq2_in.at[k - 1])
    squares[...] = sq2[...] + jnp.sum(sq2_in[...], axis=0)
    for copy, when in sent:
        if when is None:
            copy.wait_send()
        else:
            pl.when(when)(copy.wait_send)


def scale_kernel(sizes, head_grad, row_grad, squares, head_update, row_update):
    sums = jnp.sum(squares[...], axis=1, keepdims=True)
    for i, (grad, update) in enumerate(((head_grad, head_update), (row_grad, row_update))):
        scale = lax.rsqrt(sums[i : i + 1, :] / sizes[i] + epsilon)
        update[...] = (grad[...] * scale).astype(jnp.bfloat16)


def fused(
    teacher_rows, teacher_gain, teacher_head, student_rows, student_gain, student_head, lengths
):
    n_dp = lax.axis_size("dp")
    tok, width = teacher_rows.shape
    voc, tf = teacher_head.shape
    ds, sf = student_rows.shape[1], student_head.shape[1]
    n_z, own = n_dp // COLS, tok // 4
    bf, f32 = jnp.bfloat16, jnp.float32
    hops = (1 + CHUNKS) * ((n_z - 1) * 4 + 3)
    copies = 3 + hops + 3 + 3 + 2 * n_z - 1 + 3 + 3 + n_dp - 1
    anywhere, vmem = pl.BlockSpec(memory_space=pl.ANY), pl.BlockSpec(memory_space=pltpu.VMEM)
    scalars = pl.BlockSpec(memory_space=pltpu.SMEM)
    grads = pl.pallas_call(
        functools.partial(step_kernel, n_dp),
        out_shape=(
            jax.ShapeDtypeStruct((voc, sf), f32),
            jax.ShapeDtypeStruct((own, ds), f32),
            jax.ShapeDtypeStruct((8, 128), f32),
        ),
        in_specs=[anywhere, vmem, anywhere, anywhere, vmem, anywhere, scalars],
        out_specs=(vmem, vmem, vmem),
        scratch_shapes=[
            pltpu.VMEM((4, tok, width), bf),
            pltpu.VMEM((4, 8, width), f32),
            pltpu.VMEM((n_dp, voc, tf), bf),
            pltpu.VMEM((n_dp, voc, sf), bf),
            pltpu.VMEM((tok, ds), bf),
            pltpu.VMEM((tok, ds), bf),
            pltpu.VMEM((4, tok, width), bf),
            pltpu.VMEM((voc, tok), f32),
            pltpu.VMEM((voc, tok), f32),
            pltpu.VMEM((voc, tok), bf),
            pltpu.VMEM((tok, voc), bf),
            pltpu.VMEM((8, tok), f32),
            pltpu.VMEM((3, 8, tok), f32),
            pltpu.VMEM((n_z, voc, sf), bf),
            pltpu.VMEM((n_z, voc, sf), bf),
            pltpu.VMEM((n_z - 1, voc, sf), bf),
            pltpu.VMEM((n_z - 1, voc, sf), bf),
            pltpu.VMEM((2, own, ds), bf),
            pltpu.VMEM((2, own, ds), bf),
            pltpu.VMEM((own, ds), bf),
            pltpu.VMEM((own, ds), bf),
            pltpu.VMEM((8, 128), f32),
            pltpu.VMEM((3, 8, 128), f32),
            pltpu.VMEM((8, 128), f32),
            pltpu.VMEM((n_dp - 1, 8, 128), f32),
            pltpu.SemaphoreType.DMA((copies,)),
            pltpu.SemaphoreType.DMA((copies,)),
            pltpu.SemaphoreType.DMA((4,)),
        ],
        compiler_params=pltpu.CompilerParams(
            collective_id=0, has_side_effects=True, vmem_limit_bytes=56 << 20
        ),
    )(
        teacher_rows,
        teacher_gain,
        teacher_head,
        student_rows,
        student_gain,
        student_head,
        lengths,
    )
    devices = 4 * n_dp
    return pl.pallas_call(
        functools.partial(scale_kernel, (voc * sf * devices, own * ds * devices)),
        out_shape=(
            jax.ShapeDtypeStruct((voc, sf), bf),
            jax.ShapeDtypeStruct((own, ds), bf),
        ),
        in_specs=[vmem, vmem, vmem],
        out_specs=(vmem, vmem),
        compiler_params=pltpu.CompilerParams(vmem_limit_bytes=56 << 20),
    )(*grads)


def step(*args):
    t_rows, _, t_head, s_rows, _, s_head, lengths = args
    fits = (
        (lax.axis_size("group"), lax.axis_size("mp"), lax.axis_size("dp") % COLS) == (2, 2, 0)
        and 4 * COLS <= lax.axis_size("dp") <= 16
        and t_head.shape[1] % 128 == 0
        and s_head.shape[1] % 128 == 0
        and t_rows.shape[1] % t_head.shape[1] == 0
        and t_head.shape[0] % (16 * CHUNKS) == 0
        and s_rows.shape[0] % 128 == 0
        and lengths.shape[0] == 1
    )
    return fused(*args) if fits else body(*args)


def solution(mesh):
    placed = (
        P("dp", ("group", "mp")),
        P(("group", "mp")),
        P(("group", "mp"), "dp"),
        P("dp", None),
        P(),
        P(("group", "mp"), "dp"),
        P("dp"),
    )
    return jax.shard_map(
        step,
        mesh=mesh,
        in_specs=placed,
        out_specs=(P(("group", "mp"), "dp"), P(("dp", "group", "mp"), None)),
        check_vma=False,
    )
```

```python
import functools

import jax
import jax.numpy as jnp
from jax import lax
from jax.experimental import pallas as pl
from jax.experimental.pallas import tpu as pltpu
from jax.sharding import PartitionSpec as P

DT = 5120
LMAX = 640


epsilon = 1e-06


def normalize(rows, gain):
    values = rows.astype(jnp.float32)
    mean_square = jnp.mean(values * values, axis=-1, keepdims=True)
    return (values * lax.rsqrt(mean_square + epsilon) * gain.astype(jnp.float32)).astype(
        jnp.bfloat16
    )


def against(rows, weights):
    return lax.dot_general(
        rows, weights, (((1,), (1,)), ((), ())), preferred_element_type=jnp.float32
    )


def body(
    teacher_rows, teacher_gain, teacher_head, student_rows, student_gain, student_head, lengths
):
    head_teacher, head_student = (
        lax.all_gather(teacher_head, "dp", axis=1, tiled=True),
        lax.all_gather(student_head, "dp", axis=1, tiled=True),
    )
    student_normed = normalize(student_rows, student_gain)
    tokens = student_rows.shape[0]
    values = teacher_rows.astype(jnp.float32)
    squares = lax.psum(jnp.sum(values * values, axis=1), ("group", "mp"))
    scale = lax.rsqrt(squares / DT + epsilon)
    teacher_normed = (values * scale[:, None] * teacher_gain.astype(jnp.float32)).astype(
        jnp.bfloat16
    )
    teacher_logits = against(
        lax.all_gather(teacher_normed, ("group", "mp"), axis=1, tiled=True), head_teacher
    )
    student_logits = against(student_normed, head_student)
    teacher_top, student_top = lax.pmax(
        (jnp.max(teacher_logits, axis=1), jnp.max(student_logits, axis=1)), ("group", "mp")
    )
    teacher_sum, student_sum = lax.psum(
        (
            jnp.sum(jnp.exp(teacher_logits - teacher_top[:, None]), axis=1),
            jnp.sum(jnp.exp(student_logits - student_top[:, None]), axis=1),
        ),
        ("group", "mp"),
    )
    teacher_lse = teacher_top + jnp.log(teacher_sum)
    student_lse = student_top + jnp.log(student_sum)
    position = jnp.arange(tokens, dtype=jnp.int32) % LMAX
    live = (position < jnp.repeat(lengths, LMAX, total_repeat_length=tokens)).astype(jnp.float32)
    teacher_prob = jnp.exp(teacher_logits - teacher_lse[:, None])
    student_prob = jnp.exp(student_logits - student_lse[:, None])
    logit_grad = (live[:, None] * (student_prob - teacher_prob)).astype(jnp.bfloat16)
    head_grad = (
        lax.psum_scatter(
            lax.dot_general(
                student_normed,
                logit_grad,
                (((0,), (0,)), ((), ())),
                preferred_element_type=jnp.float32,
            ).astype(jnp.bfloat16),
            "dp",
            scatter_dimension=0,
            tiled=True,
        )
        .astype(jnp.float32)
        .T
    )
    rows = lax.slice_in_dim(
        logit_grad,
        0,
        tokens // lax.axis_size(("group", "mp")) * lax.axis_size(("group", "mp")),
        axis=0,
    )
    row_grad = lax.psum_scatter(
        jnp.dot(rows, head_student, preferred_element_type=jnp.float32).astype(jnp.bfloat16),
        ("group", "mp"),
        scatter_dimension=0,
        tiled=True,
    ).astype(jnp.float32)
    devices = lax.axis_size(("dp", "group", "mp"))
    head_square, row_square = lax.psum(
        (jnp.sum(head_grad * head_grad), jnp.sum(row_grad * row_grad)), ("dp", "group", "mp")
    )
    head_update = head_grad * lax.rsqrt(head_square / (head_grad.size * devices) + epsilon)
    row_update = row_grad * lax.rsqrt(row_square / (row_grad.size * devices) + epsilon)
    return (head_update.astype(jnp.bfloat16), row_update.astype(jnp.bfloat16))


MESH = pl.DeviceIdType.MESH
COLS = 2
CHUNKS = 3


def dot_nt(a, b):
    return lax.dot_general(a, b, (((1,), (1,)), ((), ())), preferred_element_type=jnp.float32)


def step_kernel(
    n_dp,
    t_rows, t_gain, t_head, s_rows, s_gain, s_head, lengths,
    h_acc, r_acc, squares,
    rows_all, gain_all, ht, hs, srow, sn, tn, t_exp, s_exp, lg_t, lg,
    stat, stat_in, hx_out, hx_in, hz_out, hz_in,
    rc_out, rc_in, ry_out, ry_in, sq, sq_in, sq2, sq2_in,
    send_sem, recv_sem, local_sem,
):
    n_z = n_dp // COLS
    d, g, m = lax.axis_index("dp"), lax.axis_index("group"), lax.axis_index("mp")
    z, x = d // COLS, d % COLS
    px, pg, pm = 1 - x, 1 - g, 1 - m
    me = 2 * g + m
    voc, tf = t_head.shape
    sf = s_head.shape[1]
    tok, ds = s_rows.shape
    blocks = 4
    own = tok // blocks
    peers = [dict(group=g, mp=pm), dict(group=pg, mp=m), dict(group=pg, mp=pm)]
    peers_gm = [2 * g + pm, 2 * pg + m, 2 * pg + pm]

    barrier = pltpu.get_barrier_semaphore()
    for peer in peers:
        pl.semaphore_signal(barrier, inc=1, device_id=peer, device_id_type=MESH)
    for k in range(1, n_dp):
        pl.semaphore_signal(
            barrier, inc=1, device_id={"dp": (d + k) % n_dp}, device_id_type=MESH
        )

    locals_ = [
        pltpu.make_async_copy(src, dst, local_sem.at[i])
        for i, (src, dst) in enumerate(
            [
                (s_rows, srow),
                (t_rows, rows_all.at[me]),
                (t_head, ht.at[d]),
                (s_head, hs.at[d]),
            ]
        )
    ]
    for copy in locals_:
        copy.start()
    gain_all[me] = jnp.broadcast_to(
        t_gain[...].astype(jnp.float32).reshape(1, -1), gain_all.shape[1:]
    )
    pl.semaphore_wait(barrier, 3 + n_dp - 1)

    sent, always = [], None

    def send(src, dst, to, when=always):
        i = len(sent)
        copy = pltpu.make_async_remote_copy(
            src_ref=src, dst_ref=dst, send_sem=send_sem.at[i], recv_sem=recv_sem.at[i],
            device_id=to, device_id_type=MESH,
        )
        if when is None:
            copy.start()
        else:
            pl.when(when)(copy.start)
        sent.append((copy, when))
        return i

    def arrive(i, dst):
        pltpu.make_async_remote_copy(
            src_ref=dst, dst_ref=dst, send_sem=send_sem.at[i], recv_sem=recv_sem.at[i],
            device_id={"dp": d}, device_id_type=MESH,
        ).wait_recv()

    def col(k):
        return ((z + k) % n_z) * COLS + x

    to_x = {"dp": z * COLS + px}
    to_y = {"mp": pm}
    to_core = {"group": pg}
    piece = voc // CHUNKS

    def part(ref, c):
        return ref.at[pl.ds(c * piece, piece), :]

    parts = [(s_head, hs, None)] + [(t_head, ht, c) for c in range(CHUNKS)]
    ways = (1, -1)

    def view(ref, c):
        return ref if c is None else part(ref, c)

    def inside(at):
        return (at >= 0) & (at < n_z)

    along, across = {}, {}
    halves = [pl.ds(h * (tok // 2), tok // 2) for h in range(2)]
    rows_far = []
    for p, (src, dst, c) in enumerate(parts):
        for way in ways:
            along[way, 0, p] = send(
                view(src, c), view(dst.at[d], c), {"dp": (z + way) % n_z * COLS + x},
                inside(z + way),
            )
        across[p] = send(view(src, c), view(dst.at[d], c), to_x)
        if p == 0:
            rows_y = [send(t_rows.at[at, :], rows_all.at[me, at, :], to_y) for at in halves]
    rows_core = send(t_rows, rows_all.at[me], to_core)
    gains = [send(gain_all.at[me], gain_all.at[me], peer) for peer in peers]

    def origin(way, hop):
        return z - way * (hop + 1)

    def block(way, hop, column):
        return (origin(way, hop) + n_z) % n_z * COLS + column

    def forward(hop, p):
        _, dst, c = parts[p]
        for way in ways:
            here = inside(origin(way, hop))
            slot = view(dst.at[block(way, hop, x)], c)

            @pl.when(here)
            def _():
                arrive(along[way, hop, p], slot)

            if hop < n_z - 2:
                along[way, hop + 1, p] = send(
                    slot, slot, {"dp": (z + way + n_z) % n_z * COLS + x}, here & inside(z + way)
                )
            if hop == 0:
                across[way, hop, p] = send(slot, slot, to_x, here & ~from_end(way))
            elif hop < n_z - 2 or p not in bent:
                across[way, hop, p] = send(slot, slot, to_x, here)

    bent = (2, 3)
    turned, bend = {}, {}

    def from_end(way):
        return ~inside(origin(way, 0) - way)

    def arrive_if(when, i, dst):
        @pl.when(when)
        def _():
            arrive(i, dst)

    def turn(p):
        _, dst, c = parts[p]
        slot = view(dst.at[z * COLS + px], c)
        arrive(across[p], slot)
        for way in ways:
            turned[way, p] = send(
                slot, slot, {"dp": (z + way + n_z) % n_z * COLS + x},
                inside(z + way) & ~inside(z - way),
            )

    def through(hop, way):
        return inside(origin(way, hop)) & inside(z + way)

    def bend_on(p):
        _, dst, c = parts[p]
        for way in ways:
            slot = view(dst.at[block(way, n_z - 3, px)], c)
            arrive_if(through(n_z - 3, way), across[way, n_z - 3, p], slot)
            bend[way, p] = send(
                slot, slot, {"dp": (z + way + n_z) % n_z * COLS + x}, through(n_z - 3, way)
            )

    def arrive_across(way, hop, p):
        _, dst, c = parts[p]
        slot = view(dst.at[block(way, hop, px)], c)
        here = inside(origin(way, hop))
        if hop == 0:
            arrive_if(here & from_end(way), turned[way, p], slot)
            arrive_if(here & ~from_end(way), across[way, hop, p], slot)
        elif p not in bent or hop < n_z - 3:
            arrive_if(here, across[way, hop, p], slot)
        elif hop == n_z - 3:
            arrive_if(here & ~inside(z + way), across[way, hop, p], slot)
        else:
            arrive_if(here, bend[way, p], slot)

    locals_[0].wait()
    tile = 32

    gain = s_gain[...].astype(jnp.float32).reshape(1, -1)

    def student_tile(i, _):
        at = pl.ds(pl.multiple_of(i * tile, tile), tile)
        values = srow[at, :].astype(jnp.float32)
        mean_square = jnp.mean(values * values, axis=-1, keepdims=True)
        sn[at, :] = (values * lax.rsqrt(mean_square + epsilon) * gain).astype(jnp.bfloat16)
        return 0

    lax.fori_loop(0, tok // tile, student_tile, 0)

    def student_block(f):
        at = pl.ds(pl.multiple_of(f * sf, sf), sf)
        s_exp[...] += dot_nt(hs[f], sn[:, at])

    def student_blocks(which):
        def step(i, _):
            @pl.when(which(i))
            def _():
                student_block(i * COLS + x)
                student_block(i * COLS + px)

            return 0

        lax.fori_loop(0, n_z, step, 0)

    def softmax_part(ref, row):
        values = ref[...]
        top = jnp.max(values, axis=0, keepdims=True)
        exps = jnp.exp(values - top)
        ref[...] = exps
        stat[row : row + 1, :] = top
        stat[row + 1 : row + 2, :] = jnp.sum(exps, axis=0, keepdims=True)

    for hop in range(n_z - 2):
        for p in range(len(parts)):
            forward(hop, p)
            if hop == 0:
                turn(p)
        if hop < 2:
            slot = rows_all.at[peers_gm[0], halves[hop], :]
            arrive(rows_y[hop], slot)
            rows_far.append(send(slot, slot, to_core))

    near = n_z - 2
    locals_[3].wait()
    for hop in range(near):
        for way in ways:
            arrive_across(way, hop, 0)
    s_exp[...] = jnp.zeros_like(s_exp)
    student_blocks(lambda i: (i - z <= near) & (z - i <= near))
    bend_on(bent[0])
    forward(near, 0)
    forward(near, 1)
    locals_[1].wait()
    for i in range(3):
        arrive(gains[i], gain_all.at[peers_gm[i]])
    arrive(rows_core, rows_all.at[peers_gm[1]])
    for h in range(2):
        arrive(rows_far[h], rows_all.at[peers_gm[2], halves[h], :])
    width = t_rows.shape[1]

    def teacher_tile(i, _):
        at = pl.ds(pl.multiple_of(i * tile, tile), tile)
        total = jnp.zeros((tile, 1), jnp.float32)
        for j in range(blocks):
            values = rows_all[j, at, :].astype(jnp.float32)
            total += jnp.sum(values * values, axis=-1, keepdims=True)
        scale = lax.rsqrt(total / (blocks * width) + epsilon)
        for j in range(blocks):
            values = rows_all[j, at, :].astype(jnp.float32)
            tn[j, at, :] = (values * scale * gain_all[j, 0:1, :]).astype(jnp.bfloat16)
        return 0

    lax.fori_loop(0, tok // tile, teacher_tile, 0)

    bend_on(bent[1])
    for p in bent:
        forward(near, p)
    for way in ways:
        arrive_across(way, near, 0)
    student_blocks(lambda i: (i - z > near) | (z - i > near))
    stat[...] = jnp.zeros_like(stat)
    softmax_part(s_exp, 0)

    per = width // tf

    def teacher_block(f):
        at = pl.ds(pl.multiple_of((f % per) * tf, tf), tf)
        t_exp[...] += dot_nt(ht[f], tn[f // per, :, at])

    locals_[2].wait()
    t_exp[...] = jnp.zeros_like(t_exp)

    def own_column(i, _):
        teacher_block(i * COLS + x)
        return 0

    lax.fori_loop(0, n_z, own_column, 0)
    teacher_block(z * COLS + px)
    for hop in range(n_z - 1):
        for way in ways:
            for p in range(1, len(parts)):
                arrive_across(way, hop, p)

            @pl.when(inside(origin(way, hop)))
            def _():
                teacher_block(block(way, hop, px))

    softmax_part(t_exp, 2)

    stats = [send(stat, stat_in.at[i], peers[i]) for i in range(3)]
    for i in range(3):
        arrive(stats[i], stat_in.at[i])

    position = lax.broadcasted_iota(jnp.int32, (1, tok), 1) % LMAX
    live = (position < lengths[0]).astype(jnp.float32)

    def factor(row):
        tops = [stat[row : row + 1, :]] + [stat_in[i, row : row + 1, :] for i in range(3)]
        sums = [stat[row + 1 : row + 2, :]] + [
            stat_in[i, row + 1 : row + 2, :] for i in range(3)
        ]
        top = functools.reduce(jnp.maximum, tops)
        total = sum(s * jnp.exp(t - top) for s, t in zip(sums, tops))
        return live * jnp.exp(tops[0] - top - jnp.log(total))

    grad = s_exp[...] * factor(0) - t_exp[...] * factor(2)
    lg_t[...] = grad.astype(jnp.bfloat16)

    def head_block(f):
        at = pl.ds(pl.multiple_of(f * sf, sf), sf)
        return jnp.dot(lg_t[...], sn[:, at], preferred_element_type=jnp.float32)

    def row_block(t, dst, taken=None):
        at = pl.ds(pl.multiple_of(t * own, own), own)

        def step(f, _):
            to = pl.ds(pl.multiple_of(f * sf, sf), sf)
            value = jnp.dot(lg[at, :], hs[f], preferred_element_type=jnp.float32)
            if taken is not None:
                value += taken[:, to].astype(jnp.float32)
            dst[:, to] = value.astype(dst.dtype)
            return 0

        lax.fori_loop(0, n_dp, step, 0)

    def to_mate():
        at = pl.ds(pl.multiple_of(2 * pg * own, own), 2 * own)

        def step(f, _):
            to = pl.ds(pl.multiple_of(f * sf, sf), sf)
            value = jnp.dot(lg[at, :], hs[f], preferred_element_type=jnp.float32)
            value = value.astype(jnp.bfloat16)
            rc_out[0, :, to] = value[:own]
            rc_out[1, :, to] = value[own:]
            return 0

        lax.fori_loop(0, n_dp, step, 0)
        return [send(rc_out.at[mp], rc_in.at[mp], to_core) for mp in (pm, m)]

    order = [*range(1, n_z), 0]
    hx, hz = {}, {}
    for k in order:
        hx_out[k] = head_block(((z + k) % n_z) * COLS + px).astype(jnp.bfloat16)
        hx[k] = send(hx_out.at[k], hx_in.at[k], to_x)
        if k == order[0]:
            lg[...] = lg_t[...].T
            rc = to_mate()
    arrive(rc[0], rc_in.at[pm])
    row_block(2 * g + pm, ry_out, rc_in.at[pm])
    ry = send(ry_out, ry_in, to_y)
    for k in order[:-1]:
        value = head_block(col(k))
        arrive(hx[k], hx_in.at[k])
        hz_out[k - 1] = (value + hx_in[k].astype(jnp.float32)).astype(jnp.bfloat16)
        hz[k] = send(hz_out.at[k - 1], hz_in.at[k - 1], {"dp": col(k)})
    value = head_block(d)
    arrive(hx[0], hx_in.at[0])
    h_acc[...] = value + hx_in[0].astype(jnp.float32)
    arrive(rc[1], rc_in.at[m])
    row_block(2 * g + m, r_acc, rc_in.at[m])
    for k in range(1, n_z):
        arrive(hz[k], hz_in.at[k - 1])
    total = h_acc[...] + sum(hz_in[k].astype(jnp.float32) for k in range(n_z - 1))
    h_acc[...] = total

    def fold(values):
        lanes = jnp.sum(values * values, axis=0, keepdims=True)
        return sum(lanes[:, i : i + 128] for i in range(0, lanes.shape[1], 128))

    sq[...] = jnp.zeros_like(sq)
    sq[0:1, :] = fold(total)
    arrive(ry, ry_in)

    def row_sum(i, acc):
        at = pl.ds(pl.multiple_of(i * tile, tile), tile)
        values = r_acc[at, :] + ry_in[at, :].astype(jnp.float32)
        r_acc[at, :] = values
        return acc + fold(values)

    sq[1:2, :] = lax.fori_loop(0, own // tile, row_sum, jnp.zeros((1, 128), jnp.float32))

    first = [send(sq, sq_in.at[i], peers[i]) for i in range(3)]
    for i in range(3):
        arrive(first[i], sq_in.at[i])
    sq2[...] = sq[...] + sq_in[0] + sq_in[1] + sq_in[2]
    second = [send(sq2, sq2_in.at[k - 1], {"dp": (d + k) % n_dp}) for k in range(1, n_dp)]
    for k in range(1, n_dp):
        arrive(second[k - 1], sq2_in.at[k - 1])
    squares[...] = sq2[...] + jnp.sum(sq2_in[...], axis=0)
    for copy, when in sent:
        if when is None:
            copy.wait_send()
        else:
            pl.when(when)(copy.wait_send)


def scale_kernel(sizes, head_grad, row_grad, squares, head_update, row_update):
    sums = jnp.sum(squares[...], axis=1, keepdims=True)
    for i, (grad, update) in enumerate(((head_grad, head_update), (row_grad, row_update))):
        scale = lax.rsqrt(sums[i : i + 1, :] / sizes[i] + epsilon)
        update[...] = (grad[...] * scale).astype(jnp.bfloat16)


def fused(
    teacher_rows, teacher_gain, teacher_head, student_rows, student_gain, student_head, lengths
):
    n_dp = lax.axis_size("dp")
    tok, width = teacher_rows.shape
    voc, tf = teacher_head.shape
    ds, sf = student_rows.shape[1], student_head.shape[1]
    n_z, own = n_dp // COLS, tok // 4
    bf, f32 = jnp.bfloat16, jnp.float32
    hops = (1 + CHUNKS) * ((n_z - 1) * 4 + 3)
    copies = 5 + hops + 3 + 3 + 2 * n_z - 1 + 3 + 3 + n_dp - 1
    anywhere, vmem = pl.BlockSpec(memory_space=pl.ANY), pl.BlockSpec(memory_space=pltpu.VMEM)
    scalars = pl.BlockSpec(memory_space=pltpu.SMEM)
    grads = pl.pallas_call(
        functools.partial(step_kernel, n_dp),
        out_shape=(
            jax.ShapeDtypeStruct((voc, sf), f32),
            jax.ShapeDtypeStruct((own, ds), f32),
            jax.ShapeDtypeStruct((8, 128), f32),
        ),
        in_specs=[anywhere, vmem, anywhere, anywhere, vmem, anywhere, scalars],
        out_specs=(vmem, vmem, vmem),
        scratch_shapes=[
            pltpu.VMEM((4, tok, width), bf),
            pltpu.VMEM((4, 8, width), f32),
            pltpu.VMEM((n_dp, voc, tf), bf),
            pltpu.VMEM((n_dp, voc, sf), bf),
            pltpu.VMEM((tok, ds), bf),
            pltpu.VMEM((tok, ds), bf),
            pltpu.VMEM((4, tok, width), bf),
            pltpu.VMEM((voc, tok), f32),
            pltpu.VMEM((voc, tok), f32),
            pltpu.VMEM((voc, tok), bf),
            pltpu.VMEM((tok, voc), bf),
            pltpu.VMEM((8, tok), f32),
            pltpu.VMEM((3, 8, tok), f32),
            pltpu.VMEM((n_z, voc, sf), bf),
            pltpu.VMEM((n_z, voc, sf), bf),
            pltpu.VMEM((n_z - 1, voc, sf), bf),
            pltpu.VMEM((n_z - 1, voc, sf), bf),
            pltpu.VMEM((2, own, ds), bf),
            pltpu.VMEM((2, own, ds), bf),
            pltpu.VMEM((own, ds), bf),
            pltpu.VMEM((own, ds), bf),
            pltpu.VMEM((8, 128), f32),
            pltpu.VMEM((3, 8, 128), f32),
            pltpu.VMEM((8, 128), f32),
            pltpu.VMEM((n_dp - 1, 8, 128), f32),
            pltpu.SemaphoreType.DMA((copies,)),
            pltpu.SemaphoreType.DMA((copies,)),
            pltpu.SemaphoreType.DMA((4,)),
        ],
        compiler_params=pltpu.CompilerParams(
            collective_id=0, has_side_effects=True, vmem_limit_bytes=56 << 20
        ),
    )(
        teacher_rows,
        teacher_gain,
        teacher_head,
        student_rows,
        student_gain,
        student_head,
        lengths,
    )
    devices = 4 * n_dp
    return pl.pallas_call(
        functools.partial(scale_kernel, (voc * sf * devices, own * ds * devices)),
        out_shape=(
            jax.ShapeDtypeStruct((voc, sf), bf),
            jax.ShapeDtypeStruct((own, ds), bf),
        ),
        in_specs=[vmem, vmem, vmem],
        out_specs=(vmem, vmem),
        compiler_params=pltpu.CompilerParams(vmem_limit_bytes=56 << 20),
    )(*grads)


def step(*args):
    t_rows, _, t_head, s_rows, _, s_head, lengths = args
    fits = (
        (lax.axis_size("group"), lax.axis_size("mp"), lax.axis_size("dp") % COLS) == (2, 2, 0)
        and 4 * COLS <= lax.axis_size("dp") <= 16
        and t_head.shape[1] % 128 == 0
        and s_head.shape[1] % 128 == 0
        and t_rows.shape[1] % t_head.shape[1] == 0
        and t_head.shape[0] % (16 * CHUNKS) == 0
        and s_rows.shape[0] % 128 == 0
        and lengths.shape[0] == 1
    )
    return fused(*args) if fits else body(*args)


def solution(mesh):
    placed = (
        P("dp", ("group", "mp")),
        P(("group", "mp")),
        P(("group", "mp"), "dp"),
        P("dp", None),
        P(),
        P(("group", "mp"), "dp"),
        P("dp"),
    )
    return jax.shard_map(
        step,
        mesh=mesh,
        in_specs=placed,
        out_specs=(P(("group", "mp"), "dp"), P(("dp", "group", "mp"), None)),
        check_vma=False,
    )
```

```python
import functools

import jax
import jax.numpy as jnp
from jax import lax
from jax.experimental import pallas as pl
from jax.experimental.pallas import tpu as pltpu
from jax.sharding import PartitionSpec as P

DT = 5120
LMAX = 640


epsilon = 1e-06


def normalize(rows, gain):
    values = rows.astype(jnp.float32)
    mean_square = jnp.mean(values * values, axis=-1, keepdims=True)
    return (values * lax.rsqrt(mean_square + epsilon) * gain.astype(jnp.float32)).astype(
        jnp.bfloat16
    )


def against(rows, weights):
    return lax.dot_general(
        rows, weights, (((1,), (1,)), ((), ())), preferred_element_type=jnp.float32
    )


def body(
    teacher_rows, teacher_gain, teacher_head, student_rows, student_gain, student_head, lengths
):
    head_teacher, head_student = (
        lax.all_gather(teacher_head, "dp", axis=1, tiled=True),
        lax.all_gather(student_head, "dp", axis=1, tiled=True),
    )
    student_normed = normalize(student_rows, student_gain)
    tokens = student_rows.shape[0]
    values = teacher_rows.astype(jnp.float32)
    squares = lax.psum(jnp.sum(values * values, axis=1), ("group", "mp"))
    scale = lax.rsqrt(squares / DT + epsilon)
    teacher_normed = (values * scale[:, None] * teacher_gain.astype(jnp.float32)).astype(
        jnp.bfloat16
    )
    teacher_logits = against(
        lax.all_gather(teacher_normed, ("group", "mp"), axis=1, tiled=True), head_teacher
    )
    student_logits = against(student_normed, head_student)
    teacher_top, student_top = lax.pmax(
        (jnp.max(teacher_logits, axis=1), jnp.max(student_logits, axis=1)), ("group", "mp")
    )
    teacher_sum, student_sum = lax.psum(
        (
            jnp.sum(jnp.exp(teacher_logits - teacher_top[:, None]), axis=1),
            jnp.sum(jnp.exp(student_logits - student_top[:, None]), axis=1),
        ),
        ("group", "mp"),
    )
    teacher_lse = teacher_top + jnp.log(teacher_sum)
    student_lse = student_top + jnp.log(student_sum)
    position = jnp.arange(tokens, dtype=jnp.int32) % LMAX
    live = (position < jnp.repeat(lengths, LMAX, total_repeat_length=tokens)).astype(jnp.float32)
    teacher_prob = jnp.exp(teacher_logits - teacher_lse[:, None])
    student_prob = jnp.exp(student_logits - student_lse[:, None])
    logit_grad = (live[:, None] * (student_prob - teacher_prob)).astype(jnp.bfloat16)
    head_grad = (
        lax.psum_scatter(
            lax.dot_general(
                student_normed,
                logit_grad,
                (((0,), (0,)), ((), ())),
                preferred_element_type=jnp.float32,
            ).astype(jnp.bfloat16),
            "dp",
            scatter_dimension=0,
            tiled=True,
        )
        .astype(jnp.float32)
        .T
    )
    rows = lax.slice_in_dim(
        logit_grad,
        0,
        tokens // lax.axis_size(("group", "mp")) * lax.axis_size(("group", "mp")),
        axis=0,
    )
    row_grad = lax.psum_scatter(
        jnp.dot(rows, head_student, preferred_element_type=jnp.float32).astype(jnp.bfloat16),
        ("group", "mp"),
        scatter_dimension=0,
        tiled=True,
    ).astype(jnp.float32)
    devices = lax.axis_size(("dp", "group", "mp"))
    head_square, row_square = lax.psum(
        (jnp.sum(head_grad * head_grad), jnp.sum(row_grad * row_grad)), ("dp", "group", "mp")
    )
    head_update = head_grad * lax.rsqrt(head_square / (head_grad.size * devices) + epsilon)
    row_update = row_grad * lax.rsqrt(row_square / (row_grad.size * devices) + epsilon)
    return (head_update.astype(jnp.bfloat16), row_update.astype(jnp.bfloat16))


MESH = pl.DeviceIdType.MESH
COLS = 2
CHUNKS = 3


def dot_nt(a, b):
    return lax.dot_general(a, b, (((1,), (1,)), ((), ())), preferred_element_type=jnp.float32)


def step_kernel(
    n_dp,
    t_rows, t_gain, t_head, s_rows, s_gain, s_head, lengths,
    h_acc, r_acc, squares,
    rows_all, gain_all, ht, hs, srow, sn, tn, t_exp, s_exp, lg_t, lg,
    stat, stat_in, hx_out, hx_in, hz_out, hz_in,
    rc_out, rc_in, ry_out, ry_in, sq, sq_in, sq2, sq2_in,
    send_sem, recv_sem, local_sem,
):
    n_z = n_dp // COLS
    d, g, m = lax.axis_index("dp"), lax.axis_index("group"), lax.axis_index("mp")
    z, x = d // COLS, d % COLS
    px, pg, pm = 1 - x, 1 - g, 1 - m
    me = 2 * g + m
    voc, tf = t_head.shape
    sf = s_head.shape[1]
    tok, ds = s_rows.shape
    blocks = 4
    own = tok // blocks
    peers = [dict(group=g, mp=pm), dict(group=pg, mp=m), dict(group=pg, mp=pm)]
    peers_gm = [2 * g + pm, 2 * pg + m, 2 * pg + pm]

    barrier = pltpu.get_barrier_semaphore()
    for peer in peers:
        pl.semaphore_signal(barrier, inc=1, device_id=peer, device_id_type=MESH)
    for k in range(1, n_dp):
        pl.semaphore_signal(
            barrier, inc=1, device_id={"dp": (d + k) % n_dp}, device_id_type=MESH
        )

    locals_ = [
        pltpu.make_async_copy(src, dst, local_sem.at[i])
        for i, (src, dst) in enumerate(
            [
                (s_rows, srow),
                (t_rows, rows_all.at[me]),
                (t_head, ht.at[d]),
                (s_head, hs.at[d]),
            ]
        )
    ]
    for copy in locals_:
        copy.start()
    gain_all[me] = jnp.broadcast_to(
        t_gain[...].astype(jnp.float32).reshape(1, -1), gain_all.shape[1:]
    )
    pl.semaphore_wait(barrier, 3 + n_dp - 1)

    sent, always = [], None

    def send(src, dst, to, when=always):
        i = len(sent)
        copy = pltpu.make_async_remote_copy(
            src_ref=src, dst_ref=dst, send_sem=send_sem.at[i], recv_sem=recv_sem.at[i],
            device_id=to, device_id_type=MESH,
        )
        if when is None:
            copy.start()
        else:
            pl.when(when)(copy.start)
        sent.append((copy, when))
        return i

    def arrive(i, dst):
        pltpu.make_async_remote_copy(
            src_ref=dst, dst_ref=dst, send_sem=send_sem.at[i], recv_sem=recv_sem.at[i],
            device_id={"dp": d}, device_id_type=MESH,
        ).wait_recv()

    def col(k):
        return ((z + k) % n_z) * COLS + x

    to_x = {"dp": z * COLS + px}
    to_y = {"mp": pm}
    to_core = {"group": pg}
    piece = voc // CHUNKS

    def part(ref, c):
        return ref.at[pl.ds(c * piece, piece), :]

    parts = [(s_head, hs, None)] + [(t_head, ht, c) for c in range(CHUNKS)]
    ways = (1, -1)

    def view(ref, c):
        return ref if c is None else part(ref, c)

    def inside(at):
        return (at >= 0) & (at < n_z)

    along, across = {}, {}
    for p, (src, dst, c) in enumerate(parts):
        for way in ways:
            along[way, 0, p] = send(
                view(src, c), view(dst.at[d], c), {"dp": (z + way) % n_z * COLS + x},
                inside(z + way),
            )
        across[p] = send(view(src, c), view(dst.at[d], c), to_x)
        if p == 0:
            rows_y = send(t_rows, rows_all.at[me], to_y)
    rows_core = send(t_rows, rows_all.at[me], to_core)
    gains = [send(gain_all.at[me], gain_all.at[me], peer) for peer in peers]

    def origin(way, hop):
        return z - way * (hop + 1)

    def block(way, hop, column):
        return (origin(way, hop) + n_z) % n_z * COLS + column

    def forward(hop, p):
        _, dst, c = parts[p]
        for way in ways:
            here = inside(origin(way, hop))
            slot = view(dst.at[block(way, hop, x)], c)

            @pl.when(here)
            def _():
                arrive(along[way, hop, p], slot)

            if hop < n_z - 2:
                along[way, hop + 1, p] = send(
                    slot, slot, {"dp": (z + way + n_z) % n_z * COLS + x}, here & inside(z + way)
                )
            if hop == 0:
                across[way, hop, p] = send(slot, slot, to_x, here & ~from_end(way))
            elif hop < n_z - 2 or p not in bent:
                across[way, hop, p] = send(slot, slot, to_x, here)

    bent = (2, 3)
    turned, bend = {}, {}

    def from_end(way):
        return ~inside(origin(way, 0) - way)

    def arrive_if(when, i, dst):
        @pl.when(when)
        def _():
            arrive(i, dst)

    def turn(p):
        _, dst, c = parts[p]
        slot = view(dst.at[z * COLS + px], c)
        arrive(across[p], slot)
        for way in ways:
            turned[way, p] = send(
                slot, slot, {"dp": (z + way + n_z) % n_z * COLS + x},
                inside(z + way) & ~inside(z - way),
            )

    def through(hop, way):
        return inside(origin(way, hop)) & inside(z + way)

    def bend_on(p):
        _, dst, c = parts[p]
        for way in ways:
            slot = view(dst.at[block(way, n_z - 3, px)], c)
            arrive_if(through(n_z - 3, way), across[way, n_z - 3, p], slot)
            bend[way, p] = send(
                slot, slot, {"dp": (z + way + n_z) % n_z * COLS + x}, through(n_z - 3, way)
            )

    def arrive_across(way, hop, p):
        _, dst, c = parts[p]
        slot = view(dst.at[block(way, hop, px)], c)
        here = inside(origin(way, hop))
        if hop == 0:
            arrive_if(here & from_end(way), turned[way, p], slot)
            arrive_if(here & ~from_end(way), across[way, hop, p], slot)
        elif p not in bent or hop < n_z - 3:
            arrive_if(here, across[way, hop, p], slot)
        elif hop == n_z - 3:
            arrive_if(here & ~inside(z + way), across[way, hop, p], slot)
        else:
            arrive_if(here, bend[way, p], slot)

    locals_[0].wait()
    tile = 32

    gain = s_gain[...].astype(jnp.float32).reshape(1, -1)

    def student_tile(i, _):
        at = pl.ds(pl.multiple_of(i * tile, tile), tile)
        values = srow[at, :].astype(jnp.float32)
        mean_square = jnp.mean(values * values, axis=-1, keepdims=True)
        sn[at, :] = (values * lax.rsqrt(mean_square + epsilon) * gain).astype(jnp.bfloat16)
        return 0

    lax.fori_loop(0, tok // tile, student_tile, 0)

    def student_block(f):
        at = pl.ds(pl.multiple_of(f * sf, sf), sf)
        s_exp[...] += dot_nt(hs[f], sn[:, at])

    def student_blocks(which):
        def step(i, _):
            @pl.when(which(i))
            def _():
                student_block(i * COLS + x)
                student_block(i * COLS + px)

            return 0

        lax.fori_loop(0, n_z, step, 0)

    def softmax_part(ref, row):
        values = ref[...]
        top = jnp.max(values, axis=0, keepdims=True)
        exps = jnp.exp(values - top)
        ref[...] = exps
        stat[row : row + 1, :] = top
        stat[row + 1 : row + 2, :] = jnp.sum(exps, axis=0, keepdims=True)

    for hop in range(n_z - 2):
        for p in range(len(parts)):
            forward(hop, p)
            if hop == 0:
                turn(p)
    arrive(rows_y, rows_all.at[peers_gm[0]])
    rows_far = send(rows_all.at[peers_gm[0]], rows_all.at[peers_gm[0]], to_core)

    near = n_z - 2
    locals_[3].wait()
    for hop in range(near):
        for way in ways:
            arrive_across(way, hop, 0)
    s_exp[...] = jnp.zeros_like(s_exp)
    student_blocks(lambda i: (i - z <= near) & (z - i <= near))
    locals_[1].wait()
    for i in range(3):
        arrive(gains[i], gain_all.at[peers_gm[i]])
    arrive(rows_core, rows_all.at[peers_gm[1]])
    arrive(rows_far, rows_all.at[peers_gm[2]])
    width = t_rows.shape[1]

    def teacher_tile(i, _):
        at = pl.ds(pl.multiple_of(i * tile, tile), tile)
        total = jnp.zeros((tile, 1), jnp.float32)
        for j in range(blocks):
            values = rows_all[j, at, :].astype(jnp.float32)
            total += jnp.sum(values * values, axis=-1, keepdims=True)
        scale = lax.rsqrt(total / (blocks * width) + epsilon)
        for j in range(blocks):
            values = rows_all[j, at, :].astype(jnp.float32)
            tn[j, at, :] = (values * scale * gain_all[j, 0:1, :]).astype(jnp.bfloat16)
        return 0

    lax.fori_loop(0, tok // tile, teacher_tile, 0)

    for p in bent:
        bend_on(p)
    passed = [p for p in range(len(parts)) if p not in bent]
    for p in passed:
        forward(near, p)

    per = width // tf

    def teacher_block(f):
        at = pl.ds(pl.multiple_of((f % per) * tf, tf), tf)
        t_exp[...] += dot_nt(ht[f], tn[f // per, :, at])

    def teacher_column(which):
        def step(i, _):
            @pl.when(which(i))
            def _():
                teacher_block(i * COLS + x)

            return 0

        lax.fori_loop(0, n_z, step, 0)

    def teacher_across(hop):
        for way in ways:
            for p in range(1, len(parts)):
                arrive_across(way, hop, p)

            @pl.when(inside(origin(way, hop)))
            def _():
                teacher_block(block(way, hop, px))

    locals_[2].wait()
    t_exp[...] = jnp.zeros_like(t_exp)
    teacher_column(lambda i: (i - z <= near) & (z - i <= near))
    teacher_block(z * COLS + px)
    for hop in range(near):
        teacher_across(hop)
    for way in ways:
        arrive_across(way, near, 0)
    student_blocks(lambda i: (i - z > near) | (z - i > near))
    stat[...] = jnp.zeros_like(stat)
    softmax_part(s_exp, 0)
    for p in bent:
        forward(near, p)
    teacher_column(lambda i: (i - z > near) | (z - i > near))
    teacher_across(near)
    softmax_part(t_exp, 2)

    stats = [send(stat, stat_in.at[i], peers[i]) for i in range(3)]
    for i in range(3):
        arrive(stats[i], stat_in.at[i])

    position = lax.broadcasted_iota(jnp.int32, (1, tok), 1) % LMAX
    live = (position < lengths[0]).astype(jnp.float32)

    def factor(row):
        tops = [stat[row : row + 1, :]] + [stat_in[i, row : row + 1, :] for i in range(3)]
        sums = [stat[row + 1 : row + 2, :]] + [
            stat_in[i, row + 1 : row + 2, :] for i in range(3)
        ]
        top = functools.reduce(jnp.maximum, tops)
        total = sum(s * jnp.exp(t - top) for s, t in zip(sums, tops))
        return live * jnp.exp(tops[0] - top - jnp.log(total))

    grad = s_exp[...] * factor(0) - t_exp[...] * factor(2)
    lg_t[...] = grad.astype(jnp.bfloat16)

    def head_block(f):
        at = pl.ds(pl.multiple_of(f * sf, sf), sf)
        return jnp.dot(lg_t[...], sn[:, at], preferred_element_type=jnp.float32)

    def row_block(t, dst, taken=None):
        at = pl.ds(pl.multiple_of(t * own, own), own)

        def step(f, _):
            to = pl.ds(pl.multiple_of(f * sf, sf), sf)
            value = jnp.dot(lg[at, :], hs[f], preferred_element_type=jnp.float32)
            if taken is not None:
                value += taken[:, to].astype(jnp.float32)
            dst[:, to] = value.astype(dst.dtype)
            return 0

        lax.fori_loop(0, n_dp, step, 0)

    def to_mate():
        at = pl.ds(pl.multiple_of(2 * pg * own, own), 2 * own)

        def step(f, _):
            to = pl.ds(pl.multiple_of(f * sf, sf), sf)
            value = jnp.dot(lg[at, :], hs[f], preferred_element_type=jnp.float32)
            value = value.astype(jnp.bfloat16)
            rc_out[0, :, to] = value[:own]
            rc_out[1, :, to] = value[own:]
            return 0

        lax.fori_loop(0, n_dp, step, 0)
        return [send(rc_out.at[mp], rc_in.at[mp], to_core) for mp in (pm, m)]

    order = [*range(1, n_z), 0]
    hx, hz = {}, {}
    for k in order:
        hx_out[k] = head_block(((z + k) % n_z) * COLS + px).astype(jnp.bfloat16)
        hx[k] = send(hx_out.at[k], hx_in.at[k], to_x)
        if k == order[0]:
            lg[...] = lg_t[...].T
            rc = to_mate()
    arrive(rc[0], rc_in.at[pm])
    row_block(2 * g + pm, ry_out, rc_in.at[pm])
    ry = send(ry_out, ry_in, to_y)
    for k in order[:-1]:
        value = head_block(col(k))
        arrive(hx[k], hx_in.at[k])
        hz_out[k - 1] = (value + hx_in[k].astype(jnp.float32)).astype(jnp.bfloat16)
        hz[k] = send(hz_out.at[k - 1], hz_in.at[k - 1], {"dp": col(k)})
    value = head_block(d)
    arrive(hx[0], hx_in.at[0])
    h_acc[...] = value + hx_in[0].astype(jnp.float32)
    arrive(rc[1], rc_in.at[m])
    row_block(2 * g + m, r_acc, rc_in.at[m])
    for k in range(1, n_z):
        arrive(hz[k], hz_in.at[k - 1])
    total = h_acc[...] + sum(hz_in[k].astype(jnp.float32) for k in range(n_z - 1))
    h_acc[...] = total

    def fold(values):
        lanes = jnp.sum(values * values, axis=0, keepdims=True)
        return sum(lanes[:, i : i + 128] for i in range(0, lanes.shape[1], 128))

    sq[...] = jnp.zeros_like(sq)
    sq[0:1, :] = fold(total)
    arrive(ry, ry_in)

    def row_sum(i, acc):
        at = pl.ds(pl.multiple_of(i * tile, tile), tile)
        values = r_acc[at, :] + ry_in[at, :].astype(jnp.float32)
        r_acc[at, :] = values
        return acc + fold(values)

    sq[1:2, :] = lax.fori_loop(0, own // tile, row_sum, jnp.zeros((1, 128), jnp.float32))

    first = [send(sq, sq_in.at[i], peers[i]) for i in range(3)]
    for i in range(3):
        arrive(first[i], sq_in.at[i])
    sq2[...] = sq[...] + sq_in[0] + sq_in[1] + sq_in[2]
    second = [send(sq2, sq2_in.at[k - 1], {"dp": (d + k) % n_dp}) for k in range(1, n_dp)]
    for k in range(1, n_dp):
        arrive(second[k - 1], sq2_in.at[k - 1])
    squares[...] = sq2[...] + jnp.sum(sq2_in[...], axis=0)
    for copy, when in sent:
        if when is None:
            copy.wait_send()
        else:
            pl.when(when)(copy.wait_send)


def scale_kernel(sizes, head_grad, row_grad, squares, head_update, row_update):
    sums = jnp.sum(squares[...], axis=1, keepdims=True)
    for i, (grad, update) in enumerate(((head_grad, head_update), (row_grad, row_update))):
        scale = lax.rsqrt(sums[i : i + 1, :] / sizes[i] + epsilon)
        update[...] = (grad[...] * scale).astype(jnp.bfloat16)


def fused(
    teacher_rows, teacher_gain, teacher_head, student_rows, student_gain, student_head, lengths
):
    n_dp = lax.axis_size("dp")
    tok, width = teacher_rows.shape
    voc, tf = teacher_head.shape
    ds, sf = student_rows.shape[1], student_head.shape[1]
    n_z, own = n_dp // COLS, tok // 4
    bf, f32 = jnp.bfloat16, jnp.float32
    hops = (1 + CHUNKS) * ((n_z - 1) * 4 + 3)
    copies = 3 + hops + 3 + 3 + 2 * n_z - 1 + 3 + 3 + n_dp - 1
    anywhere, vmem = pl.BlockSpec(memory_space=pl.ANY), pl.BlockSpec(memory_space=pltpu.VMEM)
    scalars = pl.BlockSpec(memory_space=pltpu.SMEM)
    grads = pl.pallas_call(
        functools.partial(step_kernel, n_dp),
        out_shape=(
            jax.ShapeDtypeStruct((voc, sf), f32),
            jax.ShapeDtypeStruct((own, ds), f32),
            jax.ShapeDtypeStruct((8, 128), f32),
        ),
        in_specs=[anywhere, vmem, anywhere, anywhere, vmem, anywhere, scalars],
        out_specs=(vmem, vmem, vmem),
        scratch_shapes=[
            pltpu.VMEM((4, tok, width), bf),
            pltpu.VMEM((4, 8, width), f32),
            pltpu.VMEM((n_dp, voc, tf), bf),
            pltpu.VMEM((n_dp, voc, sf), bf),
            pltpu.VMEM((tok, ds), bf),
            pltpu.VMEM((tok, ds), bf),
            pltpu.VMEM((4, tok, width), bf),
            pltpu.VMEM((voc, tok), f32),
            pltpu.VMEM((voc, tok), f32),
            pltpu.VMEM((voc, tok), bf),
            pltpu.VMEM((tok, voc), bf),
            pltpu.VMEM((8, tok), f32),
            pltpu.VMEM((3, 8, tok), f32),
            pltpu.VMEM((n_z, voc, sf), bf),
            pltpu.VMEM((n_z, voc, sf), bf),
            pltpu.VMEM((n_z - 1, voc, sf), bf),
            pltpu.VMEM((n_z - 1, voc, sf), bf),
            pltpu.VMEM((2, own, ds), bf),
            pltpu.VMEM((2, own, ds), bf),
            pltpu.VMEM((own, ds), bf),
            pltpu.VMEM((own, ds), bf),
            pltpu.VMEM((8, 128), f32),
            pltpu.VMEM((3, 8, 128), f32),
            pltpu.VMEM((8, 128), f32),
            pltpu.VMEM((n_dp - 1, 8, 128), f32),
            pltpu.SemaphoreType.DMA((copies,)),
            pltpu.SemaphoreType.DMA((copies,)),
            pltpu.SemaphoreType.DMA((4,)),
        ],
        compiler_params=pltpu.CompilerParams(
            collective_id=0, has_side_effects=True, vmem_limit_bytes=56 << 20
        ),
    )(
        teacher_rows,
        teacher_gain,
        teacher_head,
        student_rows,
        student_gain,
        student_head,
        lengths,
    )
    devices = 4 * n_dp
    return pl.pallas_call(
        functools.partial(scale_kernel, (voc * sf * devices, own * ds * devices)),
        out_shape=(
            jax.ShapeDtypeStruct((voc, sf), bf),
            jax.ShapeDtypeStruct((own, ds), bf),
        ),
        in_specs=[vmem, vmem, vmem],
        out_specs=(vmem, vmem),
        compiler_params=pltpu.CompilerParams(vmem_limit_bytes=56 << 20),
    )(*grads)


def step(*args):
    t_rows, _, t_head, s_rows, _, s_head, lengths = args
    fits = (
        (lax.axis_size("group"), lax.axis_size("mp"), lax.axis_size("dp") % COLS) == (2, 2, 0)
        and 4 * COLS <= lax.axis_size("dp") <= 16
        and t_head.shape[1] % 128 == 0
        and s_head.shape[1] % 128 == 0
        and t_rows.shape[1] % t_head.shape[1] == 0
        and t_head.shape[0] % (16 * CHUNKS) == 0
        and s_rows.shape[0] % 128 == 0
        and lengths.shape[0] == 1
    )
    return fused(*args) if fits else body(*args)


def solution(mesh):
    placed = (
        P("dp", ("group", "mp")),
        P(("group", "mp")),
        P(("group", "mp"), "dp"),
        P("dp", None),
        P(),
        P(("group", "mp"), "dp"),
        P("dp"),
    )
    return jax.shard_map(
        step,
        mesh=mesh,
        in_specs=placed,
        out_specs=(P(("group", "mp"), "dp"), P(("dp", "group", "mp"), None)),
        check_vma=False,
    )
```
